512 devices in a mesh: grp: 32 (over y, x_hi, core), span: 16 (over z, x_lo).
Axes of the slice: x: 4 (x_hi: 2, x_lo: 2; x = x_hi * 2 + x_lo), y: 8, z: 8, core: 2. Of those that a mesh axis runs over, the one named last changes fastest.
Arguments:
- strain: bfloat16 [8192, 49152], P('grp', 'span'), may hold values from -60 to 60
- channel_map: int32 [32, 256], P('grp'), may hold values from 0 to 255, each once within a row
- bin_index: int32 [64], replicated, may hold values from 1 to 511
Outputs:
- cross_spectra: bfloat16 [3, 64, 8192, 512], P(None, 'span', 'grp')
The draws below stay inside these ranges and needn't reach their ends.
All inputs are finite; a program needn't handle non-finite values.
Results may differ from the reference program's by a relative error of at most 0.0064.
Values may be sent and summed in bfloat16 or wider, within the bound.
A program may use at most 64 MiB of HBM per device.

```python
import math
import jax
import jax.numpy as jnp
from jax import lax

CH_DEV = 256
W = 1024
ROUNDS = 3
GROUPS = 32
CHANNELS = 8192
SAMPLES = 49152
RECORD_WINDOWS = 192
NBIN = 64


def draw_strain(key, part):
    noise_key, scale_key = jax.random.split(key)
    blocks = SAMPLES // (W // 4)
    noise = jnp.clip(jax.random.normal(noise_key, (CHANNELS, blocks, W // 4), jnp.float32), -6.0, 6.0)
    levels = jnp.exp(jax.random.uniform(scale_key, (CHANNELS, blocks, 1), jnp.float32, 0.0, math.log(10.0)))
    return (noise * levels).reshape(CHANNELS, SAMPLES).astype(jnp.bfloat16)


def set_ends(result, key, least, top_value):
    place = [jax.random.randint(jax.random.fold_in(key, axis), (), 0, length) for axis, length in enumerate(result.shape)]
    longest = result.shape.index(max(result.shape))
    next_to = place[:longest] + [(place[longest] + 1) % result.shape[longest]] + place[longest + 1:]
    return result.at[tuple(place)].set(least).at[tuple(next_to)].set(top_value)


def setup_inputs(seed: int = 0) -> dict:
    key_of = jax.random.split(jax.random.key(seed), 4)
    strain = draw_strain(jax.random.fold_in(key_of[3], 71), 0)
    channel_map = jax.vmap(lambda own: jax.random.permutation(own, CH_DEV))(jax.random.split(key_of[1], GROUPS)).reshape((GROUPS, CH_DEV)).astype(jnp.int32)
    bin_index = set_ends(jax.random.randint(key_of[2], (NBIN,), 1, W // 2), jax.random.fold_in(key_of[2], 1), 1, (W // 2) - 1).astype(jnp.int32)
    return dict(strain=strain, channel_map=channel_map, bin_index=bin_index)


epsilon = 1e-06

def dft_table(bin_index, length):
    sample_ids = jnp.arange(length, dtype=jnp.int32)
    phase_int = sample_ids[:, None] * bin_index[None, :] % length
    angles = phase_int.astype(jnp.float32) * (2.0 * math.pi / length)
    hann_taper = 0.5 - 0.5 * jnp.cos(sample_ids.astype(jnp.float32) * (2.0 * math.pi / length))
    cos_sin = jnp.stack([jnp.cos(angles), -jnp.sin(angles)], axis=-1)
    return (hann_taper[:, None, None] * cos_sin).reshape(length, 2 * bin_index.shape[0]).astype(jnp.bfloat16)

def cross_block(local_block, partner, stack_scale):
    half_len = partner.shape[1] // 2
    turned = jnp.concatenate([-partner[:, half_len:], partner[:, :half_len]], axis=1)
    right_operand = jnp.concatenate([partner, turned], axis=2)
    spectral_product = jnp.einsum('swu,swe->sue', local_block.astype(jnp.float32), right_operand.astype(jnp.float32))
    return (spectral_product * stack_scale).astype(jnp.bfloat16)

def reference(strain, channel_map, bin_index):
    hop_len = W // 4
    row_permutation = (jnp.arange(GROUPS, dtype=jnp.int32)[:, None] * CH_DEV + channel_map).reshape(-1).astype(jnp.int32)
    ordered = jnp.take(strain, row_permutation, axis=0)
    padded = jnp.concatenate([ordered, jnp.zeros((CHANNELS, 3 * hop_len), strain.dtype)], axis=1)
    grouped = padded.reshape(GROUPS, CH_DEV, RECORD_WINDOWS + 3, hop_len)
    fourier_basis_matrix = dft_table(bin_index, W).reshape(4, hop_len, 2 * NBIN)

    def spectra_of(block):
        window_spectra = jnp.zeros((2 * NBIN, RECORD_WINDOWS, CH_DEV), jnp.float32)
        for quarter in range(4):
            window_spectra = window_spectra + jnp.einsum('chs,sk->khc', block[:, quarter:quarter + RECORD_WINDOWS].astype(jnp.float32), fourier_basis_matrix[quarter].astype(jnp.float32))
        values = lax.optimization_barrier(window_spectra.astype(jnp.bfloat16)).astype(jnp.float32)
        values = values.reshape(NBIN, 2, RECORD_WINDOWS, CH_DEV)
        power_mean = lax.optimization_barrier(jnp.mean(values * values, axis=(1, 2)))
        whitened = (values * lax.rsqrt(power_mean + epsilon)[:, None, None, :]).astype(jnp.bfloat16)
        return whitened.reshape(NBIN, 2 * RECORD_WINDOWS, CH_DEV)
    whitened = lax.map(spectra_of, grouped)
    stack_scale = 1.0 / math.sqrt(RECORD_WINDOWS)
    rounds_out = []
    for offset in range(1, ROUNDS + 1):
        partner = jnp.roll(whitened, -offset, axis=0)
        blocks = lax.map(lambda pair: cross_block(pair[0], pair[1], stack_scale), (whitened, partner))
        rounds_out.append(blocks.transpose(1, 0, 2, 3).reshape(NBIN, CHANNELS, 2 * CH_DEV))
    return jnp.stack(rounds_out, axis=0)
```

```python
import functools
import math

import jax
import jax.numpy as jnp
from jax import lax
from jax.experimental import pallas as pl
from jax.experimental.pallas import tpu as pltpu
from jax.sharding import PartitionSpec as P

W = 1024
HOP = W // 4
ROUNDS = 3
epsilon = 1e-06
MESH = pl.DeviceIdType.MESH
BF = jnp.bfloat16
F32 = jnp.float32

PART_WINDOWS = (8, 4)
CHUNKS = ((0, 0, 2), (0, 2, 2), (1, 0, 4))


def sin_cos(x):
    x2 = x * x
    s = x * (1.0 + x2 * (-1.0 / 6 + x2 * (1.0 / 120 + x2 * (-1.0 / 5040 + x2 * (1.0 / 362880)))))
    c = 1.0 + x2 * (-0.5 + x2 * (1.0 / 24 + x2 * (-1.0 / 720 + x2 * (1.0 / 40320 - x2 * (1.0 / 3628800)))))
    return s, c


def turned(e, s, c):
    odd = (e & 1) == 1
    cos_sign = jnp.where(((e + 1) & 2) == 0, 1.0, -1.0)
    sin_sign = jnp.where((e & 2) == 0, 1.0, -1.0)
    return jnp.where(odd, s, c) * cos_sign, jnp.where(odd, c, s) * sin_sign


def fill_basis(bin_ref, basis):
    nb = bin_ref.shape[1]
    row = lax.broadcasted_iota(jnp.int32, (nb, nb), 0)
    col = lax.broadcasted_iota(jnp.int32, (nb, nb), 1)
    bins = jnp.where(row == col, jnp.broadcast_to(bin_ref[...].astype(F32), (nb, nb)), 0.0)
    bins = jnp.sum(bins, axis=1, keepdims=True).astype(jnp.int32)
    t = lax.broadcasted_iota(jnp.int32, (nb, HOP), 1)
    bins = jnp.broadcast_to(bins, (nb, HOP))

    def parts(m):
        k = (m + 128) >> 8
        s, c = sin_cos((m - (k << 8)).astype(F32) * (2.0 * math.pi / W))
        return k, s, c

    k, s, c = parts((t * bins) & (W - 1))
    tk, ts, tc = parts(lax.broadcasted_iota(jnp.int32, (8, HOP), 1))
    for q in range(4):
        cq, sq = turned((k + q * bins) & 3, s, c)
        tq, _ = turned((tk + q) & 3, ts, tc)
        taper = (0.5 - 0.5 * tq)[:1]
        base = q * 2 * nb
        basis[base : base + nb] = (taper * cq).astype(BF)
        basis[base + nb : base + 2 * nb] = (-taper * sq).astype(BF)


def exchange(
    nz, ngrp, map_ref, bin_ref, strain_ref, slab_a, slab_b,
    basis, onehot, wacc, rows_a, rows_b, out_a, out_b, transit_a, transit_b, halo_out, halo_in,
    halo_send, halo_recv, z_send, z_recv, t_recv, x_send, m_recv, x_recv, l_send, l_recv,
):
    slabs, outs, transits = (slab_a, slab_b), (out_a, out_b), (transit_a, transit_b)
    nspan = 2 * nz
    g, s = lax.axis_index("grp"), lax.axis_index("span")
    z, lo, core = s // 2, s % 2, g % 2
    nb = bin_ref.shape[1]
    channels = strain_ref.shape[0]
    win = strain_ref.shape[1] // HOP

    def at(dg, ds):
        return {"grp": lax.rem(g + dg + ngrp, ngrp), "span": ds}

    behind = lax.rem(s + nspan - 1, nspan)
    ahead = lax.rem(s + 1, nspan)
    other = z * 2 + 1 - lo

    barrier = pltpu.get_barrier_semaphore()

    def hello(device):
        pl.semaphore_signal(barrier, inc=1, device_id=device, device_id_type=MESH)

    hello(at(0, ahead))
    hello(at(0, other))
    hello(at(2, s))
    hello(at(2, other))
    hello(at(1 + 2 * core, s))
    hello(at(1 - 2 * core, s))

    def hello_z(d, _):
        hello(at(0, lax.rem(z + d, nz) * 2 + lo))
        return 0

    lax.fori_loop(1, nz, hello_z, 0)

    fill_basis(bin_ref, basis)
    c_in = lax.broadcasted_iota(jnp.int32, (channels, channels), 0)
    onehot[...] = jnp.where(c_in == jnp.broadcast_to(map_ref[...], (channels, channels)), 1.0, 0.0).astype(BF)

    def hop(j):
        block = strain_ref[:, j * HOP : (j + 1) * HOP]
        part = lax.dot_general(
            basis[...], block, (((1,), (1,)), ((), ())), preferred_element_type=F32
        )
        for q in range(4):
            i = j - q + 3
            piece = part[q * 2 * nb : (q + 1) * 2 * nb]
            if j == 0 or q == 0:
                wacc[i] = piece
            else:
                wacc[i] = wacc[i] + piece

    for j in range(3):
        hop(j)
    halo_out[...] = wacc[0:3].astype(BF)
    pl.semaphore_wait(barrier, nz - 1 + 6)
    halo = pltpu.make_async_remote_copy(
        src_ref=halo_out, dst_ref=halo_in, send_sem=halo_send, recv_sem=halo_recv,
        device_id=at(0, behind), device_id_type=MESH,
    )
    halo.start()
    for j in range(3, win):
        hop(j)

    def arrange(part, first):
        rows, out = (rows_a, rows_b)[part], outs[part]
        per = 2 * PART_WINDOWS[part]
        for w in range(PART_WINDOWS[part]):
            for p in range(2):
                at_row = (w // 4) * 8 + p * 4 + w % 4
                piece = wacc[3 + first + w, p * nb : (p + 1) * nb, :]
                for h in range(channels // 128):
                    rows[h, pl.ds(at_row, nb, stride=per), :] = piece[:, h * 128 : (h + 1) * 128]
        by_map = jnp.concatenate([rows[h].astype(BF) for h in range(channels // 128)], axis=1)
        ordered = jnp.dot(by_map, onehot[...], preferred_element_type=F32)
        out[...] = ordered.reshape(out.shape).astype(BF)

    def to_slabs(c):
        part, n0, nn = CHUNKS[c]
        out, slab, transit = outs[part], slabs[part], transits[part]
        n = pl.ds(n0, nn)
        pltpu.make_async_copy(out.at[z, 1 - lo, n], transit.at[n, z], t_recv.at[c]).start()
        pltpu.make_async_copy(out.at[z, lo, n], slab.at[0, lo, n, z], z_recv.at[c]).start()

        def send(i, _):
            off = (i + 1) // 2
            there = lax.rem(z + nz // 2 + off * (1 - 2 * (i % 2)), nz)
            device = at(0, there * 2 + lo)
            pltpu.make_async_remote_copy(
                src_ref=out.at[there, 1 - lo, n], dst_ref=transit.at[n, z],
                send_sem=z_send.at[part], recv_sem=t_recv.at[c],
                device_id=device, device_id_type=MESH,
            ).start()
            pltpu.make_async_remote_copy(
                src_ref=out.at[there, lo, n], dst_ref=slab.at[0, lo, n, z],
                send_sem=z_send.at[part], recv_sem=z_recv.at[c],
                device_id=device, device_id_type=MESH,
            ).start()
            return 0

        lax.fori_loop(0, nz - 1, send, 0)

    def arrived(ref, sem):
        pltpu.make_async_copy(ref, ref, sem).wait()

    sent = []

    def send(src, dst, send_sem, recv_sem, device):
        copy = pltpu.make_async_remote_copy(
            src_ref=src, dst_ref=dst, send_sem=send_sem, recv_sem=recv_sem,
            device_id=device, device_id_type=MESH,
        )
        copy.start()
        sent.append(copy)

    def across(c):
        part, n0, nn = CHUNKS[c]
        slab, transit = slabs[part], transits[part]
        n = pl.ds(n0, nn)
        arrived(transit.at[n], t_recv.at[c])
        send(transit.at[n], slab.at[0, lo, n], x_send.at[c, 0], m_recv.at[c], at(0, other))
        send(transit.at[n], slab.at[2, lo, n], x_send.at[c, 1], x_recv.at[c], at(-2, other))
        arrived(slab.at[0, lo, n], z_recv.at[c])
        send(slab.at[0, lo, n], slab.at[2, lo, n], x_send.at[c, 2], x_recv.at[c], at(-2, s))

    def onward(c):
        part, n0, nn = CHUNKS[c]
        slab = slabs[part]
        n = pl.ds(n0, nn)
        arrived(slab.at[0, 1 - lo, n], m_recv.at[c])
        to = 3 - 2 * core
        send(slab.at[0, :, n], slab.at[to, :, n], l_send.at[c, 0], l_recv.at[c, to // 2], at(-to, s))
        arrived(slab.at[2, :, n], x_recv.at[c])
        to = 1 + 2 * core
        send(slab.at[2, :, n], slab.at[to, :, n], l_send.at[c, 1], l_recv.at[c, to // 2], at(2 - to, s))

    def last(c):
        part, n0, nn = CHUNKS[c]
        slab = slabs[part]
        n = pl.ds(n0, nn)
        arrived(slab.at[1, :, n], l_recv.at[c, 0])
        arrived(slab.at[3, :, n], l_recv.at[c, 1])

    arrange(0, 0)
    to_slabs(0)
    to_slabs(1)
    halo.wait()
    keep = jnp.where(s == nspan - 1, 0.0, 1.0)
    for i in range(3):
        wacc[win + i] = wacc[win + i] + halo_in[i].astype(F32) * keep
    arrange(1, PART_WINDOWS[0])
    to_slabs(2)
    for c in range(len(CHUNKS)):
        across(c)
        if c:
            onward(c - 1)
    onward(len(CHUNKS) - 1)
    for c in range(len(CHUNKS)):
        last(c)
    for part in range(2):
        arrived(outs[part].at[pl.ds(0, nz - 1)], z_send.at[part])
    for copy in sent:
        copy.wait_send()


def stacked(scale, a_ref, b_ref, o_ref):
    def whitened(slot):
        a = a_ref[slot, :, 0].astype(F32)
        b = b_ref[slot, :, 0].astype(F32)
        ch = a.shape[-1]
        v = jnp.concatenate([a.reshape(-1, ch), b.reshape(-1, ch)], axis=0)
        power = jnp.sum(v * v, axis=0, keepdims=True) * (1.0 / v.shape[0])
        return v * lax.rsqrt(power + epsilon)

    own = whitened(0).astype(BF).astype(F32)
    k, ch = own.shape
    swapped = pltpu.roll(own.reshape(k // 8, 8, ch), 4, 1)
    imag_row = lax.broadcasted_iota(jnp.int32, swapped.shape, 1) >= 4
    swapped = jnp.where(imag_row, -swapped, swapped).reshape(k, ch)
    left = jnp.concatenate([own, swapped], axis=1).astype(BF)
    for r in range(ROUNDS):
        right = whitened(1 + r).astype(BF)
        both = lax.dot_general(left, right, (((0,), (0,)), ((), ())), preferred_element_type=F32)
        both = (both * scale).astype(BF)
        o_ref[r, 0, :, :ch] = both[:ch]
        o_ref[r, 0, :, ch:] = both[ch:]


def local(strain, channel_map, bin_index):
    channels = strain.shape[0]
    nspan, ngrp = lax.axis_size("span"), lax.axis_size("grp")
    nz = nspan // 2
    nb = bin_index.shape[0]
    per = nb // nspan
    rows = [2 * w for w in PART_WINDOWS]
    win = sum(PART_WINDOWS)
    nc = len(CHUNKS)
    dma = pltpu.SemaphoreType.DMA
    vmem = pl.BlockSpec(memory_space=pltpu.VMEM)
    slabs = pl.pallas_call(
        functools.partial(exchange, nz, ngrp),
        out_shape=[jax.ShapeDtypeStruct((ROUNDS + 1, 2, per, nz, r, channels), BF) for r in rows],
        in_specs=[vmem] * 3,
        out_specs=[pl.BlockSpec(memory_space=pl.ANY)] * 2,
        scratch_shapes=[
            pltpu.VMEM((8 * nb, HOP), BF),
            pltpu.VMEM((channels, channels), BF),
            pltpu.VMEM((win + 3, 2 * nb, channels), F32),
            pltpu.VMEM((channels // 128, nb * rows[0], 128), F32),
            pltpu.VMEM((channels // 128, nb * rows[1], 128), F32),
            pltpu.VMEM((nz, 2, per, rows[0], channels), BF),
            pltpu.VMEM((nz, 2, per, rows[1], channels), BF),
            pltpu.VMEM((per, nz, rows[0], channels), BF),
            pltpu.VMEM((per, nz, rows[1], channels), BF),
            pltpu.VMEM((3, 2 * nb, channels), BF),
            pltpu.VMEM((3, 2 * nb, channels), BF),
            dma, dma, dma((2,)), dma((nc,)), dma((nc,)), dma((nc, 3)), dma((nc,)), dma((nc,)), dma((nc, 2)), dma((nc, 2)),
        ],
        compiler_params=pltpu.CompilerParams(
            collective_id=0, has_side_effects=True, vmem_limit_bytes=32 * 2**20
        ),
        name="exchange",
    )(channel_map, bin_index.reshape(1, nb), strain)

    def block(r):
        return pl.BlockSpec((ROUNDS + 1, 2, 1, nz, r, channels), lambda i: (0, 0, i, 0, 0, 0))

    return pl.pallas_call(
        functools.partial(stacked, 1.0 / math.sqrt(win * nspan)),
        grid=(per,),
        in_specs=[block(r) for r in rows],
        out_specs=pl.BlockSpec((ROUNDS, 1, channels, 2 * channels), lambda i: (0, i, 0, 0)),
        out_shape=jax.ShapeDtypeStruct((ROUNDS, per, channels, 2 * channels), BF),
        compiler_params=pltpu.CompilerParams(vmem_limit_bytes=32 * 2**20),
        name="stacked",
    )(*slabs)


def solution(mesh):
    return jax.shard_map(
        local,
        mesh=mesh,
        in_specs=(P("grp", "span"), P("grp", None), P()),
        out_specs=P(None, "span", "grp", None),
        check_vma=False,
    )
```

```python
import functools
import math

import jax
import jax.numpy as jnp
from jax import lax
from jax.experimental import pallas as pl
from jax.experimental.pallas import tpu as pltpu
from jax.sharding import PartitionSpec as P

W = 1024
HOP = W // 4
ROUNDS = 3
epsilon = 1e-06
MESH = pl.DeviceIdType.MESH
BF = jnp.bfloat16
F32 = jnp.float32

PART_WINDOWS = (8, 4)
CHUNKS = ((0, 0, 1), (0, 1, 1), (0, 2, 1), (0, 3, 1), (1, 0, 2), (1, 2, 2))


def sin_cos(x):
    x2 = x * x
    s = x * (1.0 + x2 * (-1.0 / 6 + x2 * (1.0 / 120 + x2 * (-1.0 / 5040 + x2 * (1.0 / 362880)))))
    c = 1.0 + x2 * (-0.5 + x2 * (1.0 / 24 + x2 * (-1.0 / 720 + x2 * (1.0 / 40320 - x2 * (1.0 / 3628800)))))
    return s, c


def turned(e, s, c):
    odd = (e & 1) == 1
    cos_sign = jnp.where(((e + 1) & 2) == 0, 1.0, -1.0)
    sin_sign = jnp.where((e & 2) == 0, 1.0, -1.0)
    return jnp.where(odd, s, c) * cos_sign, jnp.where(odd, c, s) * sin_sign


def fill_basis(bin_ref, basis):
    nb = bin_ref.shape[1]
    row = lax.broadcasted_iota(jnp.int32, (nb, nb), 0)
    col = lax.broadcasted_iota(jnp.int32, (nb, nb), 1)
    bins = jnp.where(row == col, jnp.broadcast_to(bin_ref[...].astype(F32), (nb, nb)), 0.0)
    bins = jnp.sum(bins, axis=1, keepdims=True).astype(jnp.int32)
    t = lax.broadcasted_iota(jnp.int32, (nb, HOP), 1)
    bins = jnp.broadcast_to(bins, (nb, HOP))

    def parts(m):
        k = (m + 128) >> 8
        s, c = sin_cos((m - (k << 8)).astype(F32) * (2.0 * math.pi / W))
        return k, s, c

    k, s, c = parts((t * bins) & (W - 1))
    tk, ts, tc = parts(lax.broadcasted_iota(jnp.int32, (8, HOP), 1))
    for q in range(4):
        cq, sq = turned((k + q * bins) & 3, s, c)
        tq, _ = turned((tk + q) & 3, ts, tc)
        taper = (0.5 - 0.5 * tq)[:1]
        base = q * 2 * nb
        basis[base : base + nb] = (taper * cq).astype(BF)
        basis[base + nb : base + 2 * nb] = (-taper * sq).astype(BF)


def exchange(
    nz, ngrp, map_hbm, bin_hbm, strain_hbm, slab_a, slab_b,
    map_ref, bin_ref, strain_ref, load_sem, basis, onehot, wacc, rows_a, rows_b, out_a, out_b, transit_a, transit_b, halo_out, halo_in,
    halo_send, halo_recv, z_send, z_recv, t_recv, x_send, m_recv, x_recv, r_send, l_send, l_recv,
):
    slabs, outs, transits = (slab_a, slab_b), (out_a, out_b), (transit_a, transit_b)
    nspan = 2 * nz
    g, s = lax.axis_index("grp"), lax.axis_index("span")
    z, lo, core = s // 2, s % 2, g % 2
    nb = bin_ref.shape[1]
    channels = strain_ref.shape[0]
    win = strain_ref.shape[1] // HOP

    loads = [
        pltpu.make_async_copy(bin_hbm, bin_ref, load_sem.at[win]),
        pltpu.make_async_copy(map_hbm, map_ref, load_sem.at[win + 1]),
    ]
    for j in range(win):
        hop_samples = (slice(None), slice(j * HOP, (j + 1) * HOP))
        loads.append(pltpu.make_async_copy(strain_hbm.at[hop_samples], strain_ref.at[hop_samples], load_sem.at[j]))
    for load in loads:
        load.start()

    def at(dg, ds):
        return {"grp": lax.rem(g + dg + 2 * ngrp, ngrp), "span": ds}

    behind = lax.rem(s + nspan - 1, nspan)
    ahead = lax.rem(s + 1, nspan)
    other = z * 2 + 1 - lo

    barrier = pltpu.get_barrier_semaphore()

    def hello(device):
        pl.semaphore_signal(barrier, inc=1, device_id=device, device_id_type=MESH)

    hello(at(0, ahead))
    hello(at(0, other))
    quarter = lax.rem(g, 4)
    relayed = jnp.where(quarter == 1, 1, 0)
    relaying = jnp.where(quarter == 3, 1, 0)
    hello(at(2 - 4 * relaying, s))
    hello(at(2 - 4 * relaying, other))

    @pl.when(relaying == 1)
    def _():
        hello(at(4, s))

    hello(at(1 + 2 * core, s))
    hello(at(1 - 2 * core, s))

    def hello_z(d, _):
        hello(at(0, lax.rem(z + d, nz) * 2 + lo))
        return 0

    lax.fori_loop(1, nz, hello_z, 0)

    loads[0].wait()
    fill_basis(bin_ref, basis)
    loads[1].wait()
    c_in = lax.broadcasted_iota(jnp.int32, (channels, channels), 0)
    onehot[...] = jnp.where(c_in == jnp.broadcast_to(map_ref[...], (channels, channels)), 1.0, 0.0).astype(BF)

    def hop(j):
        loads[2 + j].wait()
        block = strain_ref[:, j * HOP : (j + 1) * HOP]
        part = lax.dot_general(
            basis[...], block, (((1,), (1,)), ((), ())), preferred_element_type=F32
        )
        for q in range(4):
            i = j - q + 3
            piece = part[q * 2 * nb : (q + 1) * 2 * nb]
            if j == 0 or q == 0:
                wacc[i] = piece
            else:
                wacc[i] = wacc[i] + piece

    for j in range(3):
        hop(j)
    halo_out[...] = wacc[0:3].astype(BF)
    pl.semaphore_wait(barrier, nz - 1 + 6 + relaying)
    halo = pltpu.make_async_remote_copy(
        src_ref=halo_out, dst_ref=halo_in, send_sem=halo_send, recv_sem=halo_recv,
        device_id=at(0, behind), device_id_type=MESH,
    )
    halo.start()
    for j in range(3, win):
        hop(j)

    def arrange(part, first):
        rows, out = (rows_a, rows_b)[part], outs[part]
        per = 2 * PART_WINDOWS[part]
        for w in range(PART_WINDOWS[part]):
            for p in range(2):
                at_row = (w // 4) * 8 + p * 4 + w % 4
                piece = wacc[3 + first + w, p * nb : (p + 1) * nb, :]
                for h in range(channels // 128):
                    rows[h, pl.ds(at_row, nb, stride=per), :] = piece[:, h * 128 : (h + 1) * 128]
        by_map = jnp.concatenate([rows[h].astype(BF) for h in range(channels // 128)], axis=1)
        ordered = jnp.dot(by_map, onehot[...], preferred_element_type=F32)
        out[...] = ordered.reshape(out.shape).astype(BF)

    def to_slabs(c):
        part, n0, nn = CHUNKS[c]
        out, slab, transit = outs[part], slabs[part], transits[part]
        n = pl.ds(n0, nn)
        pltpu.make_async_copy(out.at[z, 1 - lo, n], transit.at[n, z], t_recv.at[c]).start()
        pltpu.make_async_copy(out.at[z, lo, n], slab.at[0, lo, n, z], z_recv.at[c]).start()

        def send(half, recv_sem, dst):
            def step(i, _):
                off = (i + 1) // 2
                there = lax.rem(z + nz // 2 + off * (1 - 2 * (i % 2)), nz)
                pltpu.make_async_remote_copy(
                    src_ref=out.at[there, half, n], dst_ref=dst,
                    send_sem=z_send.at[part], recv_sem=recv_sem,
                    device_id=at(0, there * 2 + lo), device_id_type=MESH,
                ).start()
                return 0

            lax.fori_loop(0, nz - 1, step, 0)

        send(1 - lo, t_recv.at[c], transit.at[n, z])
        send(lo, z_recv.at[c], slab.at[0, lo, n, z])

    def arrived(ref, sem):
        pltpu.make_async_copy(ref, ref, sem).wait()

    sent = []

    def send(src, dst, send_sem, recv_sem, device):
        copy = pltpu.make_async_remote_copy(
            src_ref=src, dst_ref=dst, send_sem=send_sem, recv_sem=recv_sem,
            device_id=device, device_id_type=MESH,
        )
        copy.start()
        sent.append(copy)

    def across(c):
        part, n0, nn = CHUNKS[c]
        slab, transit = slabs[part], transits[part]
        n = pl.ds(n0, nn)
        to, dg, sem = 2 + 2 * relayed, 4 * relayed - 2, x_recv.at[c, relayed]
        arrived(transit.at[n], t_recv.at[c])
        send(transit.at[n], slab.at[to, lo, n], x_send.at[c, 1], sem, at(dg, other))
        send(transit.at[n], slab.at[0, lo, n], x_send.at[c, 0], m_recv.at[c], at(0, other))
        arrived(slab.at[0, lo, n], z_recv.at[c])
        send(slab.at[0, lo, n], slab.at[to, lo, n], x_send.at[c, 2], sem, at(dg, s))

    def own_onward(c):
        part, n0, nn = CHUNKS[c]
        slab = slabs[part]
        n = pl.ds(n0, nn)

        @pl.when(relaying == 1)
        def _():
            arrived(slab.at[4, :, n], x_recv.at[c, 1])
            pltpu.make_async_remote_copy(
                src_ref=slab.at[4, :, n], dst_ref=slab.at[2, :, n],
                send_sem=r_send.at[c], recv_sem=x_recv.at[c, 0], device_id=at(-4, s), device_id_type=MESH,
            ).start()

        arrived(slab.at[0, 1 - lo, n], m_recv.at[c])
        to = 3 - 2 * core
        send(slab.at[0, :, n], slab.at[to, :, n], l_send.at[c, 0], l_recv.at[c, to // 2], at(-to, s))

    def next_onward(c):
        part, n0, nn = CHUNKS[c]
        slab = slabs[part]
        n = pl.ds(n0, nn)
        arrived(slab.at[2, :, n], x_recv.at[c, 0])
        to = 1 + 2 * core
        send(slab.at[2, :, n], slab.at[to, :, n], l_send.at[c, 1], l_recv.at[c, to // 2], at(2 - to, s))

    def last(c):
        part, n0, nn = CHUNKS[c]
        slab = slabs[part]
        n = pl.ds(n0, nn)
        arrived(slab.at[1, :, n], l_recv.at[c, 0])
        arrived(slab.at[3, :, n], l_recv.at[c, 1])

    arrange(0, 0)
    for c in range(4):
        to_slabs(c)
    halo.wait()
    keep = jnp.where(s == nspan - 1, 0.0, 1.0)
    for i in range(3):
        wacc[win + i] = wacc[win + i] + halo_in[i].astype(F32) * keep
    arrange(1, PART_WINDOWS[0])
    nc = len(CHUNKS)
    for c in range(4, nc):
        to_slabs(c)
    for c in range(nc + 2):
        if c < nc:
            across(c)
        if 1 <= c <= nc:
            own_onward(c - 1)
        if c >= 2:
            next_onward(c - 2)
    for c in range(nc):
        last(c)
    for part in range(2):
        arrived(outs[part].at[pl.ds(0, nz - 1)], z_send.at[part])
    for copy in sent:
        copy.wait_send()

    @pl.when(relaying == 1)
    def _():
        for c in range(nc):
            part, n0, nn = CHUNKS[c]
            ref = slabs[part].at[4, :, pl.ds(n0, nn)]
            arrived(ref, r_send.at[c])


def stacked(scale, a_ref, b_ref, o_ref):
    def whitened(slot):
        a = a_ref[slot, :, 0].astype(F32)
        b = b_ref[slot, :, 0].astype(F32)
        ch = a.shape[-1]
        v = jnp.concatenate([a.reshape(-1, ch), b.reshape(-1, ch)], axis=0)
        power = jnp.sum(v * v, axis=0, keepdims=True) * (1.0 / v.shape[0])
        return v * lax.rsqrt(power + epsilon)

    own = whitened(0).astype(BF).astype(F32)
    k, ch = own.shape
    swapped = pltpu.roll(own.reshape(k // 8, 8, ch), 4, 1)
    imag_row = lax.broadcasted_iota(jnp.int32, swapped.shape, 1) >= 4
    swapped = jnp.where(imag_row, -swapped, swapped).reshape(k, ch)
    left = jnp.concatenate([own, swapped], axis=1).astype(BF)
    for r in range(ROUNDS):
        right = whitened(1 + r).astype(BF)
        both = lax.dot_general(left, right, (((0,), (0,)), ((), ())), preferred_element_type=F32)
        both = (both * scale).astype(BF)
        o_ref[r, 0, :, :ch] = both[:ch]
        o_ref[r, 0, :, ch:] = both[ch:]


def local(strain, channel_map, bin_index):
    channels = strain.shape[0]
    nspan, ngrp = lax.axis_size("span"), lax.axis_size("grp")
    nz = nspan // 2
    nb = bin_index.shape[0]
    per = nb // nspan
    rows = [2 * w for w in PART_WINDOWS]
    win = sum(PART_WINDOWS)
    nc = len(CHUNKS)
    dma = pltpu.SemaphoreType.DMA
    slabs = pl.pallas_call(
        functools.partial(exchange, nz, ngrp),
        out_shape=[jax.ShapeDtypeStruct((ROUNDS + 2, 2, per, nz, r, channels), BF) for r in rows],
        in_specs=[pl.BlockSpec(memory_space=pltpu.HBM)] * 3,
        out_specs=[pl.BlockSpec(memory_space=pl.ANY)] * 2,
        scratch_shapes=[
            pltpu.VMEM((1, channels), jnp.int32),
            pltpu.VMEM((1, nb), jnp.int32),
            pltpu.VMEM((channels, strain.shape[1]), BF),
            dma((win + 2,)),
            pltpu.VMEM((8 * nb, HOP), BF),
            pltpu.VMEM((channels, channels), BF),
            pltpu.VMEM((win + 3, 2 * nb, channels), F32),
            pltpu.VMEM((channels // 128, nb * rows[0], 128), F32),
            pltpu.VMEM((channels // 128, nb * rows[1], 128), F32),
            pltpu.VMEM((nz, 2, per, rows[0], channels), BF),
            pltpu.VMEM((nz, 2, per, rows[1], channels), BF),
            pltpu.VMEM((per, nz, rows[0], channels), BF),
            pltpu.VMEM((per, nz, rows[1], channels), BF),
            pltpu.VMEM((3, 2 * nb, channels), BF),
            pltpu.VMEM((3, 2 * nb, channels), BF),
            dma, dma, dma((2,)), dma((nc,)), dma((nc,)), dma((nc, 3)), dma((nc,)), dma((nc, 2)), dma((nc,)), dma((nc, 2)), dma((nc, 2)),
        ],
        compiler_params=pltpu.CompilerParams(
            collective_id=0, has_side_effects=True, vmem_limit_bytes=32 * 2**20
        ),
        name="exchange",
    )(channel_map, bin_index.reshape(1, nb), strain)

    def block(r):
        return pl.BlockSpec((ROUNDS + 1, 2, 1, nz, r, channels), lambda i: (0, 0, i, 0, 0, 0))

    return pl.pallas_call(
        functools.partial(stacked, 1.0 / math.sqrt(win * nspan)),
        grid=(per,),
        in_specs=[block(r) for r in rows],
        out_specs=pl.BlockSpec((ROUNDS, 1, channels, 2 * channels), lambda i: (0, i, 0, 0)),
        out_shape=jax.ShapeDtypeStruct((ROUNDS, per, channels, 2 * channels), BF),
        compiler_params=pltpu.CompilerParams(vmem_limit_bytes=32 * 2**20),
        name="stacked",
    )(*slabs)


def solution(mesh):
    return jax.shard_map(
        local,
        mesh=mesh,
        in_specs=(P("grp", "span"), P("grp", None), P()),
        out_specs=P(None, "span", "grp", None),
        check_vma=False,
    )
```

```python
import functools
import math

import jax
import jax.numpy as jnp
from jax import lax
from jax.experimental import pallas as pl
from jax.experimental.pallas import tpu as pltpu
from jax.sharding import PartitionSpec as P

W = 1024
HOP = W // 4
ROUNDS = 3
epsilon = 1e-06
MESH = pl.DeviceIdType.MESH
BF = jnp.bfloat16
F32 = jnp.float32

PART_WINDOWS = (8, 4)
CHUNKS = ((0, 0, 1), (0, 1, 1), (1, 0, 2), (0, 2, 1), (0, 3, 1), (1, 2, 2))


def sin_cos(x):
    x2 = x * x
    s = x * (1.0 + x2 * (-1.0 / 6 + x2 * (1.0 / 120 + x2 * (-1.0 / 5040 + x2 * (1.0 / 362880)))))
    c = 1.0 + x2 * (-0.5 + x2 * (1.0 / 24 + x2 * (-1.0 / 720 + x2 * (1.0 / 40320 - x2 * (1.0 / 3628800)))))
    return s, c


def turned(e, s, c):
    odd = (e & 1) == 1
    cos_sign = jnp.where(((e + 1) & 2) == 0, 1.0, -1.0)
    sin_sign = jnp.where((e & 2) == 0, 1.0, -1.0)
    return jnp.where(odd, s, c) * cos_sign, jnp.where(odd, c, s) * sin_sign


def fill_basis(bin_ref, basis):
    nb = bin_ref.shape[1]
    row = lax.broadcasted_iota(jnp.int32, (nb, nb), 0)
    col = lax.broadcasted_iota(jnp.int32, (nb, nb), 1)
    bins = jnp.where(row == col, jnp.broadcast_to(bin_ref[...].astype(F32), (nb, nb)), 0.0)
    bins = jnp.sum(bins, axis=1, keepdims=True).astype(jnp.int32)
    t = lax.broadcasted_iota(jnp.int32, (nb, HOP), 1)
    bins = jnp.broadcast_to(bins, (nb, HOP))

    def parts(m):
        k = (m + 128) >> 8
        s, c = sin_cos((m - (k << 8)).astype(F32) * (2.0 * math.pi / W))
        return k, s, c

    k, s, c = parts((t * bins) & (W - 1))
    tk, ts, tc = parts(lax.broadcasted_iota(jnp.int32, (8, HOP), 1))
    for q in range(4):
        cq, sq = turned((k + q * bins) & 3, s, c)
        tq, _ = turned((tk + q) & 3, ts, tc)
        taper = (0.5 - 0.5 * tq)[:1]
        base = q * 2 * nb
        basis[base : base + nb] = (taper * cq).astype(BF)
        basis[base + nb : base + 2 * nb] = (-taper * sq).astype(BF)


def exchange(
    nz, ngrp, map_hbm, bin_hbm, strain_hbm, left_hbm, right_hbm,
    slab_a, slab_b, left_ref, right_ref, map_ref, bin_ref, strain_ref, load_sem, basis, onehot, wacc, rows_a, rows_b, out_a, out_b, transit_a, transit_b, halo_out, halo_in,
    halo_send, halo_recv, z_send, z_recv, own_sem, x_send, m_recv, x_recv, r_send, l_send, l_recv, out_sem,
):
    slabs, outs, transits = (slab_a, slab_b), (out_a, out_b), (transit_a, transit_b)
    nspan = 2 * nz
    g, s = lax.axis_index("grp"), lax.axis_index("span")
    z, lo, core = s // 2, s % 2, g % 2
    nb = bin_ref.shape[1]
    channels = strain_ref.shape[0]
    win = strain_ref.shape[1] // HOP

    loads = [
        pltpu.make_async_copy(bin_hbm, bin_ref, load_sem.at[win]),
        pltpu.make_async_copy(map_hbm, map_ref, load_sem.at[win + 1]),
    ]
    for j in range(win):
        hop_samples = (slice(None), slice(j * HOP, (j + 1) * HOP))
        loads.append(pltpu.make_async_copy(strain_hbm.at[hop_samples], strain_ref.at[hop_samples], load_sem.at[j]))
    for load in loads:
        load.start()

    def at(dg, ds):
        return {"grp": lax.rem(g + dg + 2 * ngrp, ngrp), "span": ds}

    behind = lax.rem(s + nspan - 1, nspan)
    ahead = lax.rem(s + 1, nspan)
    other = z * 2 + 1 - lo

    barrier = pltpu.get_barrier_semaphore()

    def hello(device):
        pl.semaphore_signal(barrier, inc=1, device_id=device, device_id_type=MESH)

    hello(at(0, ahead))
    hello(at(0, other))
    quarter = lax.rem(g, 4)
    relayed = jnp.where(quarter == 1, 1, 0)
    relaying = jnp.where(quarter == 3, 1, 0)
    hello(at(2 - 4 * relaying, s))
    hello(at(2 - 4 * relaying, other))

    @pl.when(relaying == 1)
    def _():
        hello(at(4, s))

    hello(at(1 + 2 * core, s))
    hello(at(1 - 2 * core, s))

    def hello_z(d, _):
        hello(at(0, lax.rem(z + d, nz) * 2 + lo))
        return 0

    lax.fori_loop(1, nz, hello_z, 0)

    loads[0].wait()
    fill_basis(bin_ref, basis)
    loads[1].wait()
    c_in = lax.broadcasted_iota(jnp.int32, (channels, channels), 0)
    onehot[...] = jnp.where(c_in == jnp.broadcast_to(map_ref[...], (channels, channels)), 1.0, 0.0).astype(BF)

    def hop(j):
        loads[2 + j].wait()
        block = strain_ref[:, j * HOP : (j + 1) * HOP]
        part = lax.dot_general(
            basis[...], block, (((1,), (1,)), ((), ())), preferred_element_type=F32
        )
        for q in range(4):
            i = j - q + 3
            piece = part[q * 2 * nb : (q + 1) * 2 * nb]
            if j == 0 or q == 0:
                wacc[i] = piece
            else:
                wacc[i] = wacc[i] + piece

    for j in range(3):
        hop(j)
    halo_out[...] = wacc[0:3].astype(BF)
    pl.semaphore_wait(barrier, nz - 1 + 6 + relaying)
    halo = pltpu.make_async_remote_copy(
        src_ref=halo_out, dst_ref=halo_in, send_sem=halo_send, recv_sem=halo_recv,
        device_id=at(0, behind), device_id_type=MESH,
    )
    halo.start()
    for j in range(3, win):
        hop(j)

    def arrange(part, first):
        rows, out = (rows_a, rows_b)[part], outs[part]
        per = 2 * PART_WINDOWS[part]
        for w in range(PART_WINDOWS[part]):
            for p in range(2):
                at_row = (w // 4) * 8 + p * 4 + w % 4
                piece = wacc[3 + first + w, p * nb : (p + 1) * nb, :]
                for h in range(channels // 128):
                    rows[h, pl.ds(at_row, nb, stride=per), :] = piece[:, h * 128 : (h + 1) * 128]
        by_map = jnp.concatenate([rows[h].astype(BF) for h in range(channels // 128)], axis=1)
        ordered = jnp.dot(by_map, onehot[...], preferred_element_type=F32)
        out[...] = ordered.reshape(out.shape).astype(BF)

    def to_slabs(c):
        part, n0, nn = CHUNKS[c]
        out, transit = outs[part], transits[part]
        n = pl.ds(n0, nn)
        pltpu.make_async_copy(out.at[z, :, n], transit.at[:, n, z], z_recv.at[c]).start()

        def step(i, _):
            off = (i + 1) // 2
            there = lax.rem(z + nz // 2 + off * (1 - 2 * (i % 2)), nz)
            pltpu.make_async_remote_copy(
                src_ref=out.at[there, :, n], dst_ref=transit.at[:, n, z],
                send_sem=z_send.at[part], recv_sem=z_recv.at[c],
                device_id=at(0, there * 2 + lo), device_id_type=MESH,
            ).start()
            return 0

        lax.fori_loop(0, nz - 1, step, 0)

    def arrived(ref, sem):
        pltpu.make_async_copy(ref, ref, sem).wait()

    sent = []

    def send(src, dst, send_sem, recv_sem, device):
        copy = pltpu.make_async_remote_copy(
            src_ref=src, dst_ref=dst, send_sem=send_sem, recv_sem=recv_sem,
            device_id=device, device_id_type=MESH,
        )
        copy.start()
        sent.append(copy)

    def across(c):
        part, n0, nn = CHUNKS[c]
        slab, transit = slabs[part], transits[part]
        n = pl.ds(n0, nn)
        to, dg, sem = 2 + 2 * relayed, 4 * relayed - 2, x_recv.at[c, relayed]
        arrived(transit.at[:, n], z_recv.at[c])
        send(transit.at[1 - lo, n], slab.at[to, lo, n], x_send.at[c, 1], sem, at(dg, other))
        send(transit.at[1 - lo, n], slab.at[0, lo, n], x_send.at[c, 0], m_recv.at[c], at(0, other))
        send(transit.at[lo, n], slab.at[to, lo, n], x_send.at[c, 2], sem, at(dg, s))
        pltpu.make_async_copy(transit.at[lo, n], slab.at[0, lo, n], own_sem.at[c]).start()

    def own_onward(c):
        part, n0, nn = CHUNKS[c]
        slab = slabs[part]
        n = pl.ds(n0, nn)

        @pl.when(relaying == 1)
        def _():
            arrived(slab.at[4, :, n], x_recv.at[c, 1])
            pltpu.make_async_remote_copy(
                src_ref=slab.at[4, :, n], dst_ref=slab.at[2, :, n],
                send_sem=r_send.at[c], recv_sem=x_recv.at[c, 0], device_id=at(-4, s), device_id_type=MESH,
            ).start()

        arrived(slab.at[0, lo, n], own_sem.at[c])
        arrived(slab.at[0, 1 - lo, n], m_recv.at[c])
        to = 3 - 2 * core
        send(slab.at[0, :, n], slab.at[to, :, n], l_send.at[c, 0], l_recv.at[c, to // 2], at(-to, s))

    def next_onward(c):
        part, n0, nn = CHUNKS[c]
        slab = slabs[part]
        n = pl.ds(n0, nn)
        arrived(slab.at[2, :, n], x_recv.at[c, 0])
        to = 1 + 2 * core
        send(slab.at[2, :, n], slab.at[to, :, n], l_send.at[c, 1], l_recv.at[c, to // 2], at(2 - to, s))

    def last(c):
        part, n0, nn = CHUNKS[c]
        slab = slabs[part]
        n = pl.ds(n0, nn)
        arrived(slab.at[1, :, n], l_recv.at[c, 0])
        arrived(slab.at[3, :, n], l_recv.at[c, 1])

    def whitened(slot, n):
        a = slab_a[slot, :, n].astype(F32)
        b = slab_b[slot, :, n].astype(F32)
        v = jnp.concatenate([a.reshape(-1, channels), b.reshape(-1, channels)], axis=0)
        power = jnp.sum(v * v, axis=0, keepdims=True) * (1.0 / v.shape[0])
        return (v * lax.rsqrt(power + epsilon)).astype(BF)

    written = []

    def put(src, dst, sem):
        copy = pltpu.make_async_copy(src, dst, sem)
        copy.start()
        written.append(copy)

    def own_bins(bins):
        for n in bins:
            own = whitened(0, n).astype(F32)
            swapped = pltpu.roll(own.reshape(-1, 8, channels), 4, 1)
            imag_row = lax.broadcasted_iota(jnp.int32, swapped.shape, 1) >= 4
            swapped = jnp.where(imag_row, -swapped, swapped).reshape(own.shape)
            left_ref[n, :channels] = own.T.astype(BF)
            left_ref[n, channels:] = swapped.T.astype(BF)
            put(left_ref.at[n], left_hbm.at[n], out_sem.at[0, n])

    def next_bins(slot, bins):
        for n in bins:
            right_ref[n, slot - 1] = whitened(slot, n)
            put(right_ref.at[n, slot - 1], right_hbm.at[n, slot - 1], out_sem.at[slot, n])

    arrange(0, 0)
    to_slabs(0)
    to_slabs(1)
    halo.wait()
    keep = jnp.where(s == nspan - 1, 0.0, 1.0)
    for i in range(3):
        wacc[win + i] = wacc[win + i] + halo_in[i].astype(F32) * keep
    arrange(1, PART_WINDOWS[0])
    to_slabs(2)
    to_slabs(3)
    across(0)
    to_slabs(4)
    across(1)
    own_onward(0)
    to_slabs(5)
    across(2)
    own_onward(1)
    next_onward(0)
    across(3)
    own_onward(2)
    next_onward(1)
    own_bins((0, 1))
    across(4)
    own_onward(3)
    next_onward(2)
    last(0)
    next_bins(2, (0, 1))
    across(5)
    own_onward(4)
    next_onward(3)
    last(1)
    last(2)
    next_bins(1, (0, 1))
    next_bins(3, (0, 1))
    own_onward(5)
    next_onward(4)
    own_bins((2, 3))
    next_onward(5)
    last(3)
    last(4)
    next_bins(2, (2, 3))
    last(5)
    next_bins(1, (2, 3))
    next_bins(3, (2, 3))
    nc = len(CHUNKS)
    for copy in written:
        copy.wait()
    for part in range(2):
        arrived(outs[part].at[pl.ds(0, nz - 1)], z_send.at[part])
    for copy in sent:
        copy.wait_send()

    @pl.when(relaying == 1)
    def _():
        for c in range(nc):
            part, n0, nn = CHUNKS[c]
            ref = slabs[part].at[4, :, pl.ds(n0, nn)]
            arrived(ref, r_send.at[c])


def stacked(scale, left_ref, right_ref, o_ref):
    ch = right_ref.shape[-1]
    for r in range(ROUNDS):
        both = jnp.dot(left_ref[0], right_ref[0, r], preferred_element_type=F32)
        both = (both * scale).astype(BF)
        o_ref[r, 0, :, :ch] = both[:ch]
        o_ref[r, 0, :, ch:] = both[ch:]


def local(strain, channel_map, bin_index):
    channels = strain.shape[0]
    nspan, ngrp = lax.axis_size("span"), lax.axis_size("grp")
    nz = nspan // 2
    nb = bin_index.shape[0]
    per = nb // nspan
    rows = [2 * w for w in PART_WINDOWS]
    win = sum(PART_WINDOWS)
    nc = len(CHUNKS)
    dma = pltpu.SemaphoreType.DMA
    depth = nspan * sum(rows)
    left, right = pl.pallas_call(
        functools.partial(exchange, nz, ngrp),
        out_shape=[
            jax.ShapeDtypeStruct((per, 2 * channels, depth), BF),
            jax.ShapeDtypeStruct((per, ROUNDS, depth, channels), BF),
        ],
        in_specs=[pl.BlockSpec(memory_space=pltpu.HBM)] * 3,
        out_specs=[pl.BlockSpec(memory_space=pl.ANY)] * 2,
        scratch_shapes=[
            pltpu.VMEM((ROUNDS + 2, 2, per, nz, rows[0], channels), BF),
            pltpu.VMEM((ROUNDS + 2, 2, per, nz, rows[1], channels), BF),
            pltpu.VMEM((per, 2 * channels, depth), BF),
            pltpu.VMEM((per, ROUNDS, depth, channels), BF),
            pltpu.VMEM((1, channels), jnp.int32),
            pltpu.VMEM((1, nb), jnp.int32),
            pltpu.VMEM((channels, strain.shape[1]), BF),
            dma((win + 2,)),
            pltpu.VMEM((8 * nb, HOP), BF),
            pltpu.VMEM((channels, channels), BF),
            pltpu.VMEM((win + 3, 2 * nb, channels), F32),
            pltpu.VMEM((channels // 128, nb * rows[0], 128), F32),
            pltpu.VMEM((channels // 128, nb * rows[1], 128), F32),
            pltpu.VMEM((nz, 2, per, rows[0], channels), BF),
            pltpu.VMEM((nz, 2, per, rows[1], channels), BF),
            pltpu.VMEM((2, per, nz, rows[0], channels), BF),
            pltpu.VMEM((2, per, nz, rows[1], channels), BF),
            pltpu.VMEM((3, 2 * nb, channels), BF),
            pltpu.VMEM((3, 2 * nb, channels), BF),
            dma, dma, dma((2,)), dma((nc,)), dma((nc,)), dma((nc, 3)), dma((nc,)), dma((nc, 2)), dma((nc,)), dma((nc, 2)), dma((nc, 2)), dma((ROUNDS + 1, per)),
        ],
        compiler_params=pltpu.CompilerParams(
            collective_id=0, has_side_effects=True, vmem_limit_bytes=58_000_000
        ),
        name="exchange",
    )(channel_map, bin_index.reshape(1, nb), strain)

    return pl.pallas_call(
        functools.partial(stacked, 1.0 / math.sqrt(win * nspan)),
        grid=(per,),
        in_specs=[
            pl.BlockSpec((1, 2 * channels, depth), lambda i: (i, 0, 0)),
            pl.BlockSpec((1, ROUNDS, depth, channels), lambda i: (i, 0, 0, 0)),
        ],
        out_specs=pl.BlockSpec((ROUNDS, 1, channels, 2 * channels), lambda i: (0, i, 0, 0)),
        out_shape=jax.ShapeDtypeStruct((ROUNDS, per, channels, 2 * channels), BF),
        compiler_params=pltpu.CompilerParams(vmem_limit_bytes=32 * 2**20),
        name="stacked",
    )(left, right)


def solution(mesh):
    return jax.shard_map(
        local,
        mesh=mesh,
        in_specs=(P("grp", "span"), P("grp", None), P()),
        out_specs=P(None, "span", "grp", None),
        check_vma=False,
    )
```

```python
import functools
import math

import jax
import jax.numpy as jnp
from jax import lax
from jax.experimental import pallas as pl
from jax.experimental.pallas import tpu as pltpu
from jax.sharding import PartitionSpec as P

W = 1024
HOP = W // 4
ROUNDS = 3
epsilon = 1e-06
MESH = pl.DeviceIdType.MESH
BF = jnp.bfloat16
F32 = jnp.float32

PART_WINDOWS = (8, 4)
CHUNKS = ((0, 0, 1), (0, 1, 1), (1, 0, 2), (0, 2, 1), (1, 2, 2), (0, 3, 1))


def sin_cos(x):
    x2 = x * x
    s = x * (1.0 + x2 * (-1.0 / 6 + x2 * (1.0 / 120 + x2 * (-1.0 / 5040 + x2 * (1.0 / 362880)))))
    c = 1.0 + x2 * (-0.5 + x2 * (1.0 / 24 + x2 * (-1.0 / 720 + x2 * (1.0 / 40320 - x2 * (1.0 / 3628800)))))
    return s, c


def turned(e, s, c):
    odd = (e & 1) == 1
    cos_sign = jnp.where(((e + 1) & 2) == 0, 1.0, -1.0)
    sin_sign = jnp.where((e & 2) == 0, 1.0, -1.0)
    return jnp.where(odd, s, c) * cos_sign, jnp.where(odd, c, s) * sin_sign


def fill_basis(bin_ref, basis):
    nb = bin_ref.shape[1]
    row = lax.broadcasted_iota(jnp.int32, (nb, nb), 0)
    col = lax.broadcasted_iota(jnp.int32, (nb, nb), 1)
    bins = jnp.where(row == col, jnp.broadcast_to(bin_ref[...].astype(F32), (nb, nb)), 0.0)
    bins = jnp.sum(bins, axis=1, keepdims=True).astype(jnp.int32)
    t = lax.broadcasted_iota(jnp.int32, (nb, HOP), 1)
    bins = jnp.broadcast_to(bins, (nb, HOP))

    def parts(m):
        k = (m + 128) >> 8
        s, c = sin_cos((m - (k << 8)).astype(F32) * (2.0 * math.pi / W))
        return k, s, c

    k, s, c = parts((t * bins) & (W - 1))
    tk, ts, tc = parts(lax.broadcasted_iota(jnp.int32, (8, HOP), 1))
    for q in range(4):
        cq, sq = turned((k + q * bins) & 3, s, c)
        tq, _ = turned((tk + q) & 3, ts, tc)
        taper = (0.5 - 0.5 * tq)[:1]
        base = q * 2 * nb
        basis[base : base + nb] = (taper * cq).astype(BF)
        basis[base + nb : base + 2 * nb] = (-taper * sq).astype(BF)


def exchange(
    nz, ngrp, map_hbm, bin_hbm, strain_hbm, cross_hbm,
    slab_a, slab_b, via_a, via_b, left_ref, cross_ref, map_ref, bin_ref, strain_ref, load_sem, basis, onehot, wacc, rows_a, rows_b, out_a, out_b, transit_a, transit_b, halo_out, halo_in,
    halo_send, halo_recv, z_send, z_recv, own_sem, x_send, m_recv, v_send, v_recv, x_recv, r_send, l_send, l_recv, out_sem,
):
    slabs, vias, outs, transits = (slab_a, slab_b), (via_a, via_b), (out_a, out_b), (transit_a, transit_b)
    nspan = 2 * nz
    scale = 1.0 / math.sqrt(nspan * (strain_ref.shape[1] // HOP))
    g, s = lax.axis_index("grp"), lax.axis_index("span")
    z, lo, core = s // 2, s % 2, g % 2
    nb = bin_ref.shape[1]
    channels = strain_ref.shape[0]
    win = strain_ref.shape[1] // HOP

    loads = [
        pltpu.make_async_copy(bin_hbm, bin_ref, load_sem.at[win]),
        pltpu.make_async_copy(map_hbm, map_ref, load_sem.at[win + 1]),
    ]
    for j in range(win):
        hop_samples = (slice(None), slice(j * HOP, (j + 1) * HOP))
        loads.append(pltpu.make_async_copy(strain_hbm.at[hop_samples], strain_ref.at[hop_samples], load_sem.at[j]))
    for load in loads:
        load.start()

    def at(dg, ds):
        return {"grp": lax.rem(g + dg + 2 * ngrp, ngrp), "span": ds}

    behind = lax.rem(s + nspan - 1, nspan)
    ahead = lax.rem(s + 1, nspan)
    other = z * 2 + 1 - lo

    barrier = pltpu.get_barrier_semaphore()

    def hello(device):
        pl.semaphore_signal(barrier, inc=1, device_id=device, device_id_type=MESH)

    hello(at(0, ahead))
    hello(at(0, other))
    quarter = lax.rem(g, 4)
    relayed = jnp.where(quarter == 1, 1, 0)
    relaying = jnp.where(quarter == 3, 1, 0)
    side = lax.rem(lo + core, 2)
    hello(at(2 - 4 * relaying, other))

    @pl.when(relaying == 1)
    def _():
        hello(at(4, s))

    hello(at(1 + 2 * core, s))
    hello(at(1 - 2 * core, s))

    def hello_z(d, _):
        hello(at(0, lax.rem(z + d, nz) * 2 + lo))
        return 0

    lax.fori_loop(1, nz, hello_z, 0)

    loads[0].wait()
    fill_basis(bin_ref, basis)
    loads[1].wait()
    c_in = lax.broadcasted_iota(jnp.int32, (channels, channels), 0)
    onehot[...] = jnp.where(c_in == jnp.broadcast_to(map_ref[...], (channels, channels)), 1.0, 0.0).astype(BF)

    def hop(j):
        loads[2 + j].wait()
        block = strain_ref[:, j * HOP : (j + 1) * HOP]
        part = lax.dot_general(
            basis[...], block, (((1,), (1,)), ((), ())), preferred_element_type=F32
        )
        for q in range(4):
            i = j - q + 3
            piece = part[q * 2 * nb : (q + 1) * 2 * nb]
            if j == 0 or q == 0:
                wacc[i] = piece
            else:
                wacc[i] = wacc[i] + piece

    for j in range(3):
        hop(j)
    halo_out[...] = wacc[0:3].astype(BF)
    pl.semaphore_wait(barrier, nz - 1 + 5 + relaying)
    halo = pltpu.make_async_remote_copy(
        src_ref=halo_out, dst_ref=halo_in, send_sem=halo_send, recv_sem=halo_recv,
        device_id=at(0, behind), device_id_type=MESH,
    )
    halo.start()
    for j in range(3, win):
        hop(j)

    def arrange(part, first):
        rows, out = (rows_a, rows_b)[part], outs[part]
        per = 2 * PART_WINDOWS[part]
        for w in range(PART_WINDOWS[part]):
            for p in range(2):
                at_row = (w // 4) * 8 + p * 4 + w % 4
                piece = wacc[3 + first + w, p * nb : (p + 1) * nb, :]
                for h in range(channels // 128):
                    rows[h, pl.ds(at_row, nb, stride=per), :] = piece[:, h * 128 : (h + 1) * 128]
        by_map = jnp.concatenate([rows[h].astype(BF) for h in range(channels // 128)], axis=1)
        ordered = jnp.dot(by_map, onehot[...], preferred_element_type=F32)
        out[...] = ordered.reshape(out.shape).astype(BF)

    def to_slabs(c):
        part, n0, nn = CHUNKS[c]
        out, transit = outs[part], transits[part]
        n = pl.ds(n0, nn)
        pltpu.make_async_copy(out.at[z, :, n], transit.at[:, n, z], z_recv.at[c]).start()

        def step(i, _):
            off = (i + 1) // 2
            there = lax.rem(z + nz // 2 + off * (1 - 2 * (i % 2)), nz)
            pltpu.make_async_remote_copy(
                src_ref=out.at[there, :, n], dst_ref=transit.at[:, n, z],
                send_sem=z_send.at[part], recv_sem=z_recv.at[c],
                device_id=at(0, there * 2 + lo), device_id_type=MESH,
            ).start()
            return 0

        lax.fori_loop(0, nz - 1, step, 0)

    def arrived(ref, sem):
        pltpu.make_async_copy(ref, ref, sem).wait()

    sent = []

    def send(src, dst, send_sem, recv_sem, device):
        copy = pltpu.make_async_remote_copy(
            src_ref=src, dst_ref=dst, send_sem=send_sem, recv_sem=recv_sem,
            device_id=device, device_id_type=MESH,
        )
        copy.start()
        sent.append(copy)

    def across(c):
        part, n0, nn = CHUNKS[c]
        slab, transit = slabs[part], transits[part]
        n = pl.ds(n0, nn)
        to, dg, sem = 2 + 2 * relayed, 4 * relayed - 2, x_recv.at[c, relayed]
        arrived(transit.at[:, n], z_recv.at[c])
        send(transit.at[1 - lo, n], slab.at[to, lo, n], x_send.at[c, 1], sem, at(dg, other))
        send(transit.at[1 - lo, n], slab.at[0, lo, n], x_send.at[c, 0], m_recv.at[c], at(0, other))
        send(transit.at[lo, n], vias[part].at[n], x_send.at[c, 2], v_recv.at[c], at(side * dg, other))
        pltpu.make_async_copy(transit.at[lo, n], slab.at[0, lo, n], own_sem.at[c]).start()

    def pass_on(c):
        part, n0, nn = CHUNKS[c]
        n = pl.ds(n0, nn)
        arrived(vias[part].at[n], v_recv.at[c])
        sem = side * relayed + (1 - side) * relaying
        send(vias[part].at[n], slabs[part].at[2 + 2 * sem, 1 - lo, n], v_send.at[c], x_recv.at[c, sem],
             at(side * (4 * relayed - 2), other))

    def relay(c):
        part, n0, nn = CHUNKS[c]
        slab = slabs[part]
        n = pl.ds(n0, nn)

        @pl.when(relaying == 1)
        def _():
            arrived(slab.at[4, :, n], x_recv.at[c, 1])
            pltpu.make_async_remote_copy(
                src_ref=slab.at[4, :, n], dst_ref=slab.at[2, :, n],
                send_sem=r_send.at[c], recv_sem=x_recv.at[c, 0], device_id=at(-4, s), device_id_type=MESH,
            ).start()

    def own_onward(c):
        part, n0, nn = CHUNKS[c]
        slab = slabs[part]
        n = pl.ds(n0, nn)
        arrived(slab.at[0, lo, n], own_sem.at[c])
        arrived(slab.at[0, 1 - lo, n], m_recv.at[c])
        to = 3 - 2 * core
        send(slab.at[0, :, n], slab.at[to, :, n], l_send.at[c, 0], l_recv.at[c, to // 2], at(-to, s))

    def next_onward(c):
        part, n0, nn = CHUNKS[c]
        slab = slabs[part]
        n = pl.ds(n0, nn)
        arrived(slab.at[2, :, n], x_recv.at[c, 0])
        to = 1 + 2 * core
        send(slab.at[2, :, n], slab.at[to, :, n], l_send.at[c, 1], l_recv.at[c, to // 2], at(2 - to, s))

    def last(c):
        part, n0, nn = CHUNKS[c]
        slab = slabs[part]
        n = pl.ds(n0, nn)
        arrived(slab.at[1, :, n], l_recv.at[c, 0])
        arrived(slab.at[3, :, n], l_recv.at[c, 1])

    def whitened(slot, n):
        a = slab_a[slot, :, n].astype(F32)
        b = slab_b[slot, :, n].astype(F32)
        v = jnp.concatenate([a.reshape(-1, channels), b.reshape(-1, channels)], axis=0)
        power = jnp.sum(v * v, axis=0, keepdims=True) * (1.0 / v.shape[0])
        return (v * lax.rsqrt(power + epsilon)).astype(BF)

    written = []

    def own_bins(*bins):
        for n in bins:
            own = whitened(0, n).astype(F32)
            swapped = pltpu.roll(own.reshape(-1, 8, channels), 4, 1)
            imag_row = lax.broadcasted_iota(jnp.int32, swapped.shape, 1) >= 4
            swapped = jnp.where(imag_row, -swapped, swapped).reshape(own.shape)
            left_ref[n, :channels] = own.T.astype(BF)
            left_ref[n, channels:] = swapped.T.astype(BF)

    def stack_bins(slot, *bins):
        for n in bins:
            both = jnp.dot(left_ref[n], whitened(slot, n), preferred_element_type=F32)
            both = (both * scale).astype(BF)
            cross_ref[slot - 1, n, :, :channels] = both[:channels]
            cross_ref[slot - 1, n, :, channels:] = both[channels:]
            copy = pltpu.make_async_copy(
                cross_ref.at[slot - 1, n], cross_hbm.at[slot - 1, n], out_sem.at[slot - 1, n]
            )
            copy.start()
            written.append(copy)

    arrange(0, 0)
    to_slabs(0)
    to_slabs(1)
    halo.wait()
    keep = jnp.where(s == nspan - 1, 0.0, 1.0)
    for i in range(3):
        wacc[win + i] = wacc[win + i] + halo_in[i].astype(F32) * keep
    arrange(1, PART_WINDOWS[0])
    to_slabs(2)
    to_slabs(3)
    across(0)
    to_slabs(4)
    across(1)
    to_slabs(5)
    pass_on(0)
    own_onward(0)
    across(2)
    pass_on(1)
    own_onward(1)
    relay(0)
    across(3)
    pass_on(2)
    own_onward(2)
    relay(1)
    next_onward(0)
    own_bins(0, 1)
    across(4)
    pass_on(3)
    own_onward(3)
    relay(2)
    next_onward(1)
    across(5)
    pass_on(4)
    own_onward(4)
    relay(3)
    next_onward(2)
    own_bins(2)
    stack_bins(2, 0, 1)
    pass_on(5)
    own_onward(5)
    relay(4)
    next_onward(3)
    last(0)
    last(1)
    last(2)
    stack_bins(1, 0, 1)
    stack_bins(3, 0, 1)
    relay(5)
    next_onward(4)
    own_bins(3)
    next_onward(5)
    stack_bins(2, 2)
    last(3)
    last(4)
    stack_bins(1, 2)
    stack_bins(3, 2)
    stack_bins(2, 3)
    last(5)
    stack_bins(1, 3)
    stack_bins(3, 3)
    nc = len(CHUNKS)
    for copy in written:
        copy.wait()
    for part in range(2):
        arrived(outs[part].at[pl.ds(0, nz - 1)], z_send.at[part])
    for copy in sent:
        copy.wait_send()

    @pl.when(relaying == 1)
    def _():
        for c in range(nc):
            part, n0, nn = CHUNKS[c]
            ref = slabs[part].at[4, :, pl.ds(n0, nn)]
            arrived(ref, r_send.at[c])


def local(strain, channel_map, bin_index):
    channels = strain.shape[0]
    nspan, ngrp = lax.axis_size("span"), lax.axis_size("grp")
    nz = nspan // 2
    nb = bin_index.shape[0]
    per = nb // nspan
    rows = [2 * w for w in PART_WINDOWS]
    win = sum(PART_WINDOWS)
    nc = len(CHUNKS)
    dma = pltpu.SemaphoreType.DMA
    depth = nspan * sum(rows)
    return pl.pallas_call(
        functools.partial(exchange, nz, ngrp),
        out_shape=jax.ShapeDtypeStruct((ROUNDS, per, channels, 2 * channels), BF),
        in_specs=[pl.BlockSpec(memory_space=pltpu.HBM)] * 3,
        out_specs=pl.BlockSpec(memory_space=pl.ANY),
        scratch_shapes=[
            pltpu.VMEM((ROUNDS + 2, 2, per, nz, rows[0], channels), BF),
            pltpu.VMEM((ROUNDS + 2, 2, per, nz, rows[1], channels), BF),
            pltpu.VMEM((per, nz, rows[0], channels), BF),
            pltpu.VMEM((per, nz, rows[1], channels), BF),
            pltpu.VMEM((per, 2 * channels, depth), BF),
            pltpu.VMEM((ROUNDS, per, channels, 2 * channels), BF),
            pltpu.VMEM((1, channels), jnp.int32),
            pltpu.VMEM((1, nb), jnp.int32),
            pltpu.VMEM((channels, strain.shape[1]), BF),
            dma((win + 2,)),
            pltpu.VMEM((8 * nb, HOP), BF),
            pltpu.VMEM((channels, channels), BF),
            pltpu.VMEM((win + 3, 2 * nb, channels), F32),
            pltpu.VMEM((channels // 128, nb * rows[0], 128), F32),
            pltpu.VMEM((channels // 128, nb * rows[1], 128), F32),
            pltpu.VMEM((nz, 2, per, rows[0], channels), BF),
            pltpu.VMEM((nz, 2, per, rows[1], channels), BF),
            pltpu.VMEM((2, per, nz, rows[0], channels), BF),
            pltpu.VMEM((2, per, nz, rows[1], channels), BF),
            pltpu.VMEM((3, 2 * nb, channels), BF),
            pltpu.VMEM((3, 2 * nb, channels), BF),
            dma, dma, dma((2,)), dma((nc,)), dma((nc,)), dma((nc, 3)), dma((nc,)), dma((nc,)), dma((nc,)), dma((nc, 2)), dma((nc,)), dma((nc, 2)), dma((nc, 2)), dma((ROUNDS, per)),
        ],
        compiler_params=pltpu.CompilerParams(
            collective_id=0, has_side_effects=True, vmem_limit_bytes=58_000_000
        ),
        name="exchange",
    )(channel_map, bin_index.reshape(1, nb), strain)


def solution(mesh):
    return jax.shard_map(
        local,
        mesh=mesh,
        in_specs=(P("grp", "span"), P("grp", None), P()),
        out_specs=P(None, "span", "grp", None),
        check_vma=False,
    )
```

```python
import functools
import math

import jax
import jax.numpy as jnp
from jax import lax
from jax.experimental import pallas as pl
from jax.experimental.pallas import tpu as pltpu
from jax.sharding import PartitionSpec as P

W = 1024
HOP = W // 4
ROUNDS = 3
epsilon = 1e-06
MESH = pl.DeviceIdType.MESH
BF = jnp.bfloat16
F32 = jnp.float32

PART_WINDOWS = (8, 4)
CHUNKS = ((0, 0, 1), (0, 1, 1), (1, 0, 2), (0, 2, 1), (1, 2, 2), (0, 3, 1))


def sin_cos(x):
    x2 = x * x
    s = x * (1.0 + x2 * (-1.0 / 6 + x2 * (1.0 / 120 + x2 * (-1.0 / 5040 + x2 * (1.0 / 362880)))))
    c = 1.0 + x2 * (-0.5 + x2 * (1.0 / 24 + x2 * (-1.0 / 720 + x2 * (1.0 / 40320 - x2 * (1.0 / 3628800)))))
    return s, c


def turned(e, s, c):
    odd = (e & 1) == 1
    cos_sign = jnp.where(((e + 1) & 2) == 0, 1.0, -1.0)
    sin_sign = jnp.where((e & 2) == 0, 1.0, -1.0)
    return jnp.where(odd, s, c) * cos_sign, jnp.where(odd, c, s) * sin_sign


def fill_basis(bin_ref, basis):
    nb = bin_ref.shape[1]
    row = lax.broadcasted_iota(jnp.int32, (nb, nb), 0)
    col = lax.broadcasted_iota(jnp.int32, (nb, nb), 1)
    bins = jnp.where(row == col, jnp.broadcast_to(bin_ref[...].astype(F32), (nb, nb)), 0.0)
    bins = jnp.sum(bins, axis=1, keepdims=True).astype(jnp.int32)
    t = lax.broadcasted_iota(jnp.int32, (nb, HOP), 1)
    bins = jnp.broadcast_to(bins, (nb, HOP))

    def parts(m):
        k = (m + 128) >> 8
        s, c = sin_cos((m - (k << 8)).astype(F32) * (2.0 * math.pi / W))
        return k, s, c

    k, s, c = parts((t * bins) & (W - 1))
    tk, ts, tc = parts(lax.broadcasted_iota(jnp.int32, (8, HOP), 1))
    for q in range(4):
        cq, sq = turned((k + q * bins) & 3, s, c)
        tq, _ = turned((tk + q) & 3, ts, tc)
        taper = (0.5 - 0.5 * tq)[:1]
        base = q * 2 * nb
        basis[base : base + nb] = (taper * cq).astype(BF)
        basis[base + nb : base + 2 * nb] = (-taper * sq).astype(BF)


def exchange(
    nz, ngrp, map_hbm, bin_hbm, strain_hbm, left_ref, right_ref,
    slab_a, slab_b, map_ref, bin_ref, strain_ref, load_sem, basis, onehot, wacc, rows_a, rows_b, out_a, out_b, transit_a, transit_b, halo_out, halo_in,
    halo_send, halo_recv, z_send, z_recv, own_sem, x_send, m_recv, x_recv, r_send, l_send, l_recv,
):
    slabs, outs, transits = (slab_a, slab_b), (out_a, out_b), (transit_a, transit_b)
    nspan = 2 * nz
    g, s = lax.axis_index("grp"), lax.axis_index("span")
    z, lo, core = s // 2, s % 2, g % 2
    nb = bin_ref.shape[1]
    channels = strain_ref.shape[0]
    win = strain_ref.shape[1] // HOP

    loads = [
        pltpu.make_async_copy(bin_hbm, bin_ref, load_sem.at[win]),
        pltpu.make_async_copy(map_hbm, map_ref, load_sem.at[win + 1]),
    ]
    for j in range(win):
        hop_samples = (slice(None), slice(j * HOP, (j + 1) * HOP))
        loads.append(pltpu.make_async_copy(strain_hbm.at[hop_samples], strain_ref.at[hop_samples], load_sem.at[j]))
    for load in loads:
        load.start()

    def at(dg, ds):
        return {"grp": lax.rem(g + dg + 2 * ngrp, ngrp), "span": ds}

    behind = lax.rem(s + nspan - 1, nspan)
    ahead = lax.rem(s + 1, nspan)
    other = z * 2 + 1 - lo

    barrier = pltpu.get_barrier_semaphore()

    def hello(device):
        pl.semaphore_signal(barrier, inc=1, device_id=device, device_id_type=MESH)

    hello(at(0, ahead))
    hello(at(0, other))
    quarter = lax.rem(g, 4)
    relayed = jnp.where(quarter == 1, 1, 0)
    relaying = jnp.where(quarter == 3, 1, 0)
    hello(at(2 - 4 * relaying, s))
    hello(at(2 - 4 * relaying, other))

    @pl.when(relaying == 1)
    def _():
        hello(at(4, s))

    hello(at(1 + 2 * core, s))
    hello(at(1 - 2 * core, s))

    def hello_z(d, _):
        hello(at(0, lax.rem(z + d, nz) * 2 + lo))
        return 0

    lax.fori_loop(1, nz, hello_z, 0)

    loads[0].wait()
    fill_basis(bin_ref, basis)
    loads[1].wait()
    c_in = lax.broadcasted_iota(jnp.int32, (channels, channels), 0)
    onehot[...] = jnp.where(c_in == jnp.broadcast_to(map_ref[...], (channels, channels)), 1.0, 0.0).astype(BF)

    def hop(j):
        loads[2 + j].wait()
        block = strain_ref[:, j * HOP : (j + 1) * HOP]
        part = lax.dot_general(
            basis[...], block, (((1,), (1,)), ((), ())), preferred_element_type=F32
        )
        for q in range(4):
            i = j - q + 3
            piece = part[q * 2 * nb : (q + 1) * 2 * nb]
            if j == 0 or q == 0:
                wacc[i] = piece
            else:
                wacc[i] = wacc[i] + piece

    for j in range(3):
        hop(j)
    halo_out[...] = wacc[0:3].astype(BF)
    pl.semaphore_wait(barrier, nz - 1 + 6 + relaying)
    halo = pltpu.make_async_remote_copy(
        src_ref=halo_out, dst_ref=halo_in, send_sem=halo_send, recv_sem=halo_recv,
        device_id=at(0, behind), device_id_type=MESH,
    )
    halo.start()
    for j in range(3, win):
        hop(j)

    def arrange(part, first):
        rows, out = (rows_a, rows_b)[part], outs[part]
        per = 2 * PART_WINDOWS[part]
        for w in range(PART_WINDOWS[part]):
            for p in range(2):
                at_row = (w // 4) * 8 + p * 4 + w % 4
                piece = wacc[3 + first + w, p * nb : (p + 1) * nb, :]
                for h in range(channels // 128):
                    rows[h, pl.ds(at_row, nb, stride=per), :] = piece[:, h * 128 : (h + 1) * 128]
        by_map = jnp.concatenate([rows[h].astype(BF) for h in range(channels // 128)], axis=1)
        ordered = jnp.dot(by_map, onehot[...], preferred_element_type=F32)
        out[...] = ordered.reshape(out.shape).astype(BF)

    def to_slabs(c):
        part, n0, nn = CHUNKS[c]
        out, transit = outs[part], transits[part]
        n = pl.ds(n0, nn)
        pltpu.make_async_copy(out.at[z, :, n], transit.at[:, n, z], z_recv.at[c]).start()

        def step(i, _):
            there = i + jnp.where(i >= z, 1, 0)
            pltpu.make_async_remote_copy(
                src_ref=out.at[there, :, n], dst_ref=transit.at[:, n, z],
                send_sem=z_send.at[part], recv_sem=z_recv.at[c],
                device_id=at(0, there * 2 + lo), device_id_type=MESH,
            ).start()
            return 0

        lax.fori_loop(0, nz - 1, step, 0)

    def arrived(ref, sem):
        pltpu.make_async_copy(ref, ref, sem).wait()

    sent = []

    def send(src, dst, send_sem, recv_sem, device):
        copy = pltpu.make_async_remote_copy(
            src_ref=src, dst_ref=dst, send_sem=send_sem, recv_sem=recv_sem,
            device_id=device, device_id_type=MESH,
        )
        copy.start()
        sent.append(copy)

    def across(c):
        part, n0, nn = CHUNKS[c]
        slab, transit = slabs[part], transits[part]
        n = pl.ds(n0, nn)
        to, dg, sem = 2 + 2 * relayed, 4 * relayed - 2, x_recv.at[c, relayed]
        arrived(transit.at[:, n], z_recv.at[c])
        send(transit.at[1 - lo, n], slab.at[to, lo, n], x_send.at[c, 1], sem, at(dg, other))
        send(transit.at[1 - lo, n], slab.at[0, lo, n], x_send.at[c, 0], m_recv.at[c], at(0, other))
        send(transit.at[lo, n], slab.at[to, lo, n], x_send.at[c, 2], sem, at(dg, s))
        pltpu.make_async_copy(transit.at[lo, n], slab.at[0, lo, n], own_sem.at[c]).start()

    def relay(c):
        part, n0, nn = CHUNKS[c]
        slab = slabs[part]
        n = pl.ds(n0, nn)

        @pl.when(relaying == 1)
        def _():
            arrived(slab.at[4, :, n], x_recv.at[c, 1])
            pltpu.make_async_remote_copy(
                src_ref=slab.at[4, :, n], dst_ref=slab.at[2, :, n],
                send_sem=r_send.at[c], recv_sem=x_recv.at[c, 0], device_id=at(-4, s), device_id_type=MESH,
            ).start()

    def own_onward(c):
        part, n0, nn = CHUNKS[c]
        slab = slabs[part]
        n = pl.ds(n0, nn)
        arrived(slab.at[0, lo, n], own_sem.at[c])
        arrived(slab.at[0, 1 - lo, n], m_recv.at[c])
        to = 3 - 2 * core
        send(slab.at[0, :, n], slab.at[to, :, n], l_send.at[c, 0], l_recv.at[c, to // 2], at(-to, s))

    def next_onward(c):
        part, n0, nn = CHUNKS[c]
        slab = slabs[part]
        n = pl.ds(n0, nn)
        arrived(slab.at[2, :, n], x_recv.at[c, 0])
        to = 1 + 2 * core
        send(slab.at[2, :, n], slab.at[to, :, n], l_send.at[c, 1], l_recv.at[c, to // 2], at(2 - to, s))

    def last(c):
        part, n0, nn = CHUNKS[c]
        slab = slabs[part]
        n = pl.ds(n0, nn)
        arrived(slab.at[1, :, n], l_recv.at[c, 0])
        arrived(slab.at[3, :, n], l_recv.at[c, 1])

    def whitened(slot, n):
        a = slab_a[slot, :, n].astype(F32)
        b = slab_b[slot, :, n].astype(F32)
        v = jnp.concatenate([a.reshape(-1, channels), b.reshape(-1, channels)], axis=0)
        power = jnp.sum(v * v, axis=0, keepdims=True) * (1.0 / v.shape[0])
        return (v * lax.rsqrt(power + epsilon)).astype(BF)

    def own_bins(*bins):
        for n in bins:
            own = whitened(0, n).astype(F32)
            swapped = pltpu.roll(own.reshape(-1, 8, channels), 4, 1)
            imag_row = lax.broadcasted_iota(jnp.int32, swapped.shape, 1) >= 4
            swapped = jnp.where(imag_row, -swapped, swapped).reshape(own.shape)
            left_ref[n, :channels] = own.T.astype(BF)
            left_ref[n, channels:] = swapped.T.astype(BF)

    def next_bins(slot, *bins):
        for n in bins:
            right_ref[n, slot - 1] = whitened(slot, n)

    arrange(0, 0)
    to_slabs(0)
    to_slabs(1)
    halo.wait()
    keep = jnp.where(s == nspan - 1, 0.0, 1.0)
    for i in range(3):
        wacc[win + i] = wacc[win + i] + halo_in[i].astype(F32) * keep
    arrange(1, PART_WINDOWS[0])
    to_slabs(2)
    to_slabs(3)
    across(0)
    to_slabs(4)
    across(1)
    to_slabs(5)
    own_onward(0)
    across(2)
    own_onward(1)
    relay(0)
    across(3)
    own_onward(2)
    relay(1)
    next_onward(0)
    own_bins(0, 1)
    across(4)
    own_onward(3)
    relay(2)
    next_onward(1)
    across(5)
    own_onward(4)
    relay(3)
    next_onward(2)
    own_bins(2)
    next_bins(2, 0, 1)
    own_onward(5)
    relay(4)
    next_onward(3)
    last(0)
    last(1)
    last(2)
    next_bins(1, 0, 1)
    next_bins(3, 0, 1)
    relay(5)
    next_onward(4)
    own_bins(3)
    next_onward(5)
    next_bins(2, 2)
    last(3)
    last(4)
    next_bins(1, 2)
    next_bins(3, 2)
    next_bins(2, 3)
    last(5)
    next_bins(1, 3)
    next_bins(3, 3)
    nc = len(CHUNKS)
    for part in range(2):
        arrived(outs[part].at[pl.ds(0, nz - 1)], z_send.at[part])
    for copy in sent:
        copy.wait_send()

    @pl.when(relaying == 1)
    def _():
        for c in range(nc):
            part, n0, nn = CHUNKS[c]
            ref = slabs[part].at[4, :, pl.ds(n0, nn)]
            arrived(ref, r_send.at[c])


def stacked(scale, left_ref, right_ref, cross_hbm, cross_ref, sem):
    bins, ch = right_ref.shape[0], right_ref.shape[-1]
    copies = []
    for n in range(bins):
        for r in range(ROUNDS):
            both = jnp.dot(left_ref[n], right_ref[n, r], preferred_element_type=F32)
            both = (both * scale).astype(BF)
            cross_ref[r, n, :, :ch] = both[:ch]
            cross_ref[r, n, :, ch:] = both[ch:]
            copy = pltpu.make_async_copy(cross_ref.at[r, n], cross_hbm.at[r, n], sem.at[r, n])
            copy.start()
            copies.append(copy)
    for copy in copies:
        copy.wait()


def local(strain, channel_map, bin_index):
    channels = strain.shape[0]
    nspan, ngrp = lax.axis_size("span"), lax.axis_size("grp")
    nz = nspan // 2
    nb = bin_index.shape[0]
    per = nb // nspan
    rows = [2 * w for w in PART_WINDOWS]
    win = sum(PART_WINDOWS)
    nc = len(CHUNKS)
    dma = pltpu.SemaphoreType.DMA
    depth = nspan * sum(rows)
    left, right = pl.pallas_call(
        functools.partial(exchange, nz, ngrp),
        out_shape=[
            pltpu.VMEM((per, 2 * channels, depth), BF),
            pltpu.VMEM((per, ROUNDS, depth, channels), BF),
        ],
        in_specs=[pl.BlockSpec(memory_space=pltpu.HBM)] * 3,
        out_specs=[pl.BlockSpec(memory_space=pltpu.VMEM)] * 2,
        scratch_shapes=[
            pltpu.VMEM((ROUNDS + 2, 2, per, nz, rows[0], channels), BF),
            pltpu.VMEM((ROUNDS + 2, 2, per, nz, rows[1], channels), BF),
            pltpu.VMEM((1, channels), jnp.int32),
            pltpu.VMEM((1, nb), jnp.int32),
            pltpu.VMEM((channels, strain.shape[1]), BF),
            dma((win + 2,)),
            pltpu.VMEM((8 * nb, HOP), BF),
            pltpu.VMEM((channels, channels), BF),
            pltpu.VMEM((win + 3, 2 * nb, channels), F32),
            pltpu.VMEM((channels // 128, nb * rows[0], 128), F32),
            pltpu.VMEM((channels // 128, nb * rows[1], 128), F32),
            pltpu.VMEM((nz, 2, per, rows[0], channels), BF),
            pltpu.VMEM((nz, 2, per, rows[1], channels), BF),
            pltpu.VMEM((2, per, nz, rows[0], channels), BF),
            pltpu.VMEM((2, per, nz, rows[1], channels), BF),
            pltpu.VMEM((3, 2 * nb, channels), BF),
            pltpu.VMEM((3, 2 * nb, channels), BF),
            dma, dma, dma((2,)), dma((nc,)), dma((nc,)), dma((nc, 3)), dma((nc,)), dma((nc, 2)), dma((nc,)), dma((nc, 2)), dma((nc, 2)),
        ],
        compiler_params=pltpu.CompilerParams(
            collective_id=0, has_side_effects=True, vmem_limit_bytes=53_000_000
        ),
        name="exchange",
    )(channel_map, bin_index.reshape(1, nb), strain)

    result = (ROUNDS, per, channels, 2 * channels)
    return pl.pallas_call(
        functools.partial(stacked, 1.0 / math.sqrt(win * nspan)),
        in_specs=[pl.BlockSpec(memory_space=pltpu.VMEM)] * 2,
        out_specs=pl.BlockSpec(memory_space=pl.ANY),
        out_shape=jax.ShapeDtypeStruct(result, BF),
        scratch_shapes=[pltpu.VMEM(result, BF), dma((ROUNDS, per))],
        compiler_params=pltpu.CompilerParams(vmem_limit_bytes=32 * 2**20),
        name="stacked",
    )(left, right)


def solution(mesh):
    return jax.shard_map(
        local,
        mesh=mesh,
        in_specs=(P("grp", "span"), P("grp", None), P()),
        out_specs=P(None, "span", "grp", None),
        check_vma=False,
    )
```

```python
import functools
import math

import jax
import jax.numpy as jnp
from jax import lax
from jax.experimental import pallas as pl
from jax.experimental.pallas import tpu as pltpu
from jax.sharding import PartitionSpec as P

W = 1024
HOP = W // 4
ROUNDS = 3
epsilon = 1e-06
MESH = pl.DeviceIdType.MESH
BF = jnp.bfloat16
F32 = jnp.float32

PART_WINDOWS = (8, 4)
CHUNKS = ((0, 0, 1), (0, 1, 1), (1, 0, 2), (0, 2, 1), (1, 2, 2), (0, 3, 1))


def sin_cos(x):
    x2 = x * x
    s = x * (1.0 + x2 * (-1.0 / 6 + x2 * (1.0 / 120 + x2 * (-1.0 / 5040 + x2 * (1.0 / 362880)))))
    c = 1.0 + x2 * (-0.5 + x2 * (1.0 / 24 + x2 * (-1.0 / 720 + x2 * (1.0 / 40320 - x2 * (1.0 / 3628800)))))
    return s, c


def turned(e, s, c):
    odd = (e & 1) == 1
    cos_sign = jnp.where(((e + 1) & 2) == 0, 1.0, -1.0)
    sin_sign = jnp.where((e & 2) == 0, 1.0, -1.0)
    return jnp.where(odd, s, c) * cos_sign, jnp.where(odd, c, s) * sin_sign


def fill_basis(bin_ref, basis, nspan):
    nb = bin_ref.shape[1]
    row = lax.broadcasted_iota(jnp.int32, (nb, nb), 0)
    col = lax.broadcasted_iota(jnp.int32, (nb, nb), 1)
    row = lax.rem(row, nspan) * (nb // nspan) + row // nspan
    bins = jnp.where(row == col, jnp.broadcast_to(bin_ref[...].astype(F32), (nb, nb)), 0.0)
    bins = jnp.sum(bins, axis=1, keepdims=True).astype(jnp.int32)
    t = lax.broadcasted_iota(jnp.int32, (nb, HOP), 1)
    bins = jnp.broadcast_to(bins, (nb, HOP))

    def parts(m):
        k = (m + 128) >> 8
        s, c = sin_cos((m - (k << 8)).astype(F32) * (2.0 * math.pi / W))
        return k, s, c

    k, s, c = parts((t * bins) & (W - 1))
    tk, ts, tc = parts(lax.broadcasted_iota(jnp.int32, (8, HOP), 1))
    for q in range(4):
        cq, sq = turned((k + q * bins) & 3, s, c)
        tq, _ = turned((tk + q) & 3, ts, tc)
        taper = (0.5 - 0.5 * tq)[:1]
        base = q * 2 * nb
        basis[base : base + nb] = (taper * cq).astype(BF)
        basis[base + nb : base + 2 * nb] = (-taper * sq).astype(BF)


def exchange(
    nz, ngrp, map_hbm, bin_hbm, strain_hbm, left_ref, right_ref,
    slab_a, slab_b, map_ref, bin_ref, strain_ref, load_sem, basis, onehot, wacc, rows_a, rows_b, out_a, out_b, transit_a, transit_b, halo_out, halo_in,
    halo_send, halo_recv, z_send, z_recv, own_sem, x_send, m_recv, x_recv, r_send, l_send, l_recv,
):
    slabs, outs, transits = (slab_a, slab_b), (out_a, out_b), (transit_a, transit_b)
    nspan = 2 * nz
    g, s = lax.axis_index("grp"), lax.axis_index("span")
    z, lo, core = s // 2, s % 2, g % 2
    nb = bin_ref.shape[1]
    channels = strain_ref.shape[0]
    win = strain_ref.shape[1] // HOP

    loads = [
        pltpu.make_async_copy(bin_hbm, bin_ref, load_sem.at[win]),
        pltpu.make_async_copy(map_hbm, map_ref, load_sem.at[win + 1]),
    ]
    for j in range(win):
        hop_samples = (slice(None), slice(j * HOP, (j + 1) * HOP))
        loads.append(pltpu.make_async_copy(strain_hbm.at[hop_samples], strain_ref.at[hop_samples], load_sem.at[j]))
    for load in loads:
        load.start()

    def at(dg, ds):
        return {"grp": lax.rem(g + dg + 2 * ngrp, ngrp), "span": ds}

    behind = lax.rem(s + nspan - 1, nspan)
    ahead = lax.rem(s + 1, nspan)
    other = z * 2 + 1 - lo

    barrier = pltpu.get_barrier_semaphore()

    def hello(device):
        pl.semaphore_signal(barrier, inc=1, device_id=device, device_id_type=MESH)

    hello(at(0, ahead))
    hello(at(0, other))
    quarter = lax.rem(g, 4)
    relayed = jnp.where(quarter == 1, 1, 0)
    relaying = jnp.where(quarter == 3, 1, 0)
    hello(at(2 - 4 * relaying, s))
    hello(at(2 - 4 * relaying, other))

    @pl.when(relaying == 1)
    def _():
        hello(at(4, s))

    hello(at(1 + 2 * core, s))
    hello(at(1 - 2 * core, s))

    def hello_z(d, _):
        hello(at(0, lax.rem(z + d, nz) * 2 + lo))
        return 0

    lax.fori_loop(1, nz, hello_z, 0)

    loads[0].wait()
    fill_basis(bin_ref, basis, nspan)

    def hop(j):
        loads[2 + j].wait()
        block = strain_ref[:, j * HOP : (j + 1) * HOP]
        part = lax.dot_general(
            basis[...], block, (((1,), (1,)), ((), ())), preferred_element_type=F32
        )
        for q in range(4):
            i = j - q + 3
            piece = part[q * 2 * nb : (q + 1) * 2 * nb]
            if j == 0 or q == 0:
                wacc[i] = piece
            else:
                wacc[i] = wacc[i] + piece

    for j in range(3):
        hop(j)
    halo_out[...] = wacc[0:3].astype(BF)
    pl.semaphore_wait(barrier, nz - 1 + 6 + relaying)
    halo = pltpu.make_async_remote_copy(
        src_ref=halo_out, dst_ref=halo_in, send_sem=halo_send, recv_sem=halo_recv,
        device_id=at(0, behind), device_id_type=MESH,
    )
    halo.start()
    loads[1].wait()
    c_in = lax.broadcasted_iota(jnp.int32, (channels, channels), 0)
    onehot[...] = jnp.where(c_in == jnp.broadcast_to(map_ref[...], (channels, channels)), 1.0, 0.0).astype(BF)
    for j in range(3, win):
        hop(j)

    def arrange(part, first, n):
        rows, out = (rows_a, rows_b)[part], outs[part]
        per = 2 * PART_WINDOWS[part]
        base = n * nspan * per
        for w in range(PART_WINDOWS[part]):
            for p in range(2):
                at_row = base + (w // 4) * 8 + p * 4 + w % 4
                k = p * nb + n * nspan
                piece = wacc[3 + first + w, k : k + nspan, :]
                for h in range(channels // 128):
                    rows[h, pl.ds(at_row, nspan, stride=per), :] = piece[:, h * 128 : (h + 1) * 128]
        by_map = jnp.concatenate(
            [rows[h, base : base + nspan * per].astype(BF) for h in range(channels // 128)], axis=1
        )
        ordered = jnp.dot(by_map, onehot[...], preferred_element_type=F32)
        out[:, :, n] = ordered.reshape(nz, 2, per, channels).astype(BF)

    def to_slabs(c):
        part, n0, nn = CHUNKS[c]
        out, transit = outs[part], transits[part]
        n = pl.ds(n0, nn)
        pltpu.make_async_copy(out.at[z, :, n], transit.at[:, n, z], z_recv.at[c]).start()

        def step(i, _):
            there = i + jnp.where(i >= z, 1, 0)
            pltpu.make_async_remote_copy(
                src_ref=out.at[there, :, n], dst_ref=transit.at[:, n, z],
                send_sem=z_send.at[part], recv_sem=z_recv.at[c],
                device_id=at(0, there * 2 + lo), device_id_type=MESH,
            ).start()
            return 0

        lax.fori_loop(0, nz - 1, step, 0)

    def arrived(ref, sem):
        pltpu.make_async_copy(ref, ref, sem).wait()

    sent = []

    def send(src, dst, send_sem, recv_sem, device):
        copy = pltpu.make_async_remote_copy(
            src_ref=src, dst_ref=dst, send_sem=send_sem, recv_sem=recv_sem,
            device_id=device, device_id_type=MESH,
        )
        copy.start()
        sent.append(copy)

    def across(c):
        part, n0, nn = CHUNKS[c]
        slab, transit = slabs[part], transits[part]
        n = pl.ds(n0, nn)
        to, dg, sem = 2 + 2 * relayed, 4 * relayed - 2, x_recv.at[c, relayed]
        arrived(transit.at[:, n], z_recv.at[c])
        send(transit.at[1 - lo, n], slab.at[to, lo, n], x_send.at[c, 1], sem, at(dg, other))
        send(transit.at[1 - lo, n], slab.at[0, lo, n], x_send.at[c, 0], m_recv.at[c], at(0, other))
        send(transit.at[lo, n], slab.at[to, lo, n], x_send.at[c, 2], sem, at(dg, s))
        pltpu.make_async_copy(transit.at[lo, n], slab.at[0, lo, n], own_sem.at[c]).start()

    def relay(c):
        part, n0, nn = CHUNKS[c]
        slab = slabs[part]
        n = pl.ds(n0, nn)

        @pl.when(relaying == 1)
        def _():
            arrived(slab.at[4, :, n], x_recv.at[c, 1])
            pltpu.make_async_remote_copy(
                src_ref=slab.at[4, :, n], dst_ref=slab.at[2, :, n],
                send_sem=r_send.at[c], recv_sem=x_recv.at[c, 0], device_id=at(-4, s), device_id_type=MESH,
            ).start()

    def own_onward(c):
        part, n0, nn = CHUNKS[c]
        slab = slabs[part]
        n = pl.ds(n0, nn)
        arrived(slab.at[0, lo, n], own_sem.at[c])
        arrived(slab.at[0, 1 - lo, n], m_recv.at[c])
        to = 3 - 2 * core
        send(slab.at[0, :, n], slab.at[to, :, n], l_send.at[c, 0], l_recv.at[c, to // 2], at(-to, s))

    def next_onward(c):
        part, n0, nn = CHUNKS[c]
        slab = slabs[part]
        n = pl.ds(n0, nn)
        arrived(slab.at[2, :, n], x_recv.at[c, 0])
        to = 1 + 2 * core
        send(slab.at[2, :, n], slab.at[to, :, n], l_send.at[c, 1], l_recv.at[c, to // 2], at(2 - to, s))

    def last(c):
        part, n0, nn = CHUNKS[c]
        slab = slabs[part]
        n = pl.ds(n0, nn)
        arrived(slab.at[1, :, n], l_recv.at[c, 0])
        arrived(slab.at[3, :, n], l_recv.at[c, 1])

    def whitened(slot, n):
        a = slab_a[slot, :, n].astype(F32)
        b = slab_b[slot, :, n].astype(F32)
        v = jnp.concatenate([a.reshape(-1, channels), b.reshape(-1, channels)], axis=0)
        power = jnp.sum(v * v, axis=0, keepdims=True) * (1.0 / v.shape[0])
        return (v * lax.rsqrt(power + epsilon)).astype(BF)

    def own_bins(*bins):
        for n in bins:
            own = whitened(0, n).astype(F32)
            swapped = pltpu.roll(own.reshape(-1, 8, channels), 4, 1)
            imag_row = lax.broadcasted_iota(jnp.int32, swapped.shape, 1) >= 4
            swapped = jnp.where(imag_row, -swapped, swapped).reshape(own.shape)
            left_ref[n, :channels] = own.T.astype(BF)
            left_ref[n, channels:] = swapped.T.astype(BF)

    def next_bins(slot, *bins):
        for n in bins:
            right_ref[n, slot - 1] = whitened(slot, n)

    arrange(0, 0, 0)
    to_slabs(0)
    arrange(0, 0, 1)
    to_slabs(1)
    arrange(0, 0, 2)
    arrange(0, 0, 3)
    halo.wait()
    keep = jnp.where(s == nspan - 1, 0.0, 1.0)
    for i in range(3):
        wacc[win + i] = wacc[win + i] + halo_in[i].astype(F32) * keep
    arrange(1, PART_WINDOWS[0], 0)
    arrange(1, PART_WINDOWS[0], 1)
    to_slabs(2)
    to_slabs(3)
    arrange(1, PART_WINDOWS[0], 2)
    arrange(1, PART_WINDOWS[0], 3)
    across(0)
    to_slabs(4)
    across(1)
    to_slabs(5)
    own_onward(0)
    across(2)
    own_onward(1)
    relay(0)
    across(3)
    own_onward(2)
    relay(1)
    next_onward(0)
    own_bins(0, 1)
    across(4)
    own_onward(3)
    relay(2)
    next_onward(1)
    across(5)
    own_onward(4)
    relay(3)
    next_onward(2)
    own_bins(2)
    next_bins(2, 0, 1)
    own_onward(5)
    relay(4)
    next_onward(3)
    last(0)
    last(1)
    last(2)
    next_bins(1, 0, 1)
    next_bins(3, 0, 1)
    relay(5)
    next_onward(4)
    own_bins(3)
    next_onward(5)
    next_bins(2, 2)
    last(3)
    last(4)
    next_bins(1, 2)
    next_bins(3, 2)
    next_bins(2, 3)
    last(5)
    next_bins(1, 3)
    next_bins(3, 3)
    nc = len(CHUNKS)
    for part in range(2):
        arrived(outs[part].at[pl.ds(0, nz - 1)], z_send.at[part])
    for copy in sent:
        copy.wait_send()

    @pl.when(relaying == 1)
    def _():
        for c in range(nc):
            part, n0, nn = CHUNKS[c]
            ref = slabs[part].at[4, :, pl.ds(n0, nn)]
            arrived(ref, r_send.at[c])


def stacked(scale, left_ref, right_ref, cross_hbm, cross_ref, sem):
    bins, ch = right_ref.shape[0], right_ref.shape[-1]
    copies = []
    for n in range(bins):
        for r in range(ROUNDS):
            both = jnp.dot(left_ref[n], right_ref[n, r], preferred_element_type=F32)
            both = (both * scale).astype(BF)
            cross_ref[r, n, :, :ch] = both[:ch]
            cross_ref[r, n, :, ch:] = both[ch:]
            copy = pltpu.make_async_copy(cross_ref.at[r, n], cross_hbm.at[r, n], sem.at[r, n])
            copy.start()
            copies.append(copy)
    for copy in copies:
        copy.wait()


def local(strain, channel_map, bin_index):
    channels = strain.shape[0]
    nspan, ngrp = lax.axis_size("span"), lax.axis_size("grp")
    nz = nspan // 2
    nb = bin_index.shape[0]
    per = nb // nspan
    rows = [2 * w for w in PART_WINDOWS]
    win = sum(PART_WINDOWS)
    nc = len(CHUNKS)
    dma = pltpu.SemaphoreType.DMA
    depth = nspan * sum(rows)
    left, right = pl.pallas_call(
        functools.partial(exchange, nz, ngrp),
        out_shape=[
            pltpu.VMEM((per, 2 * channels, depth), BF),
            pltpu.VMEM((per, ROUNDS, depth, channels), BF),
        ],
        in_specs=[pl.BlockSpec(memory_space=pltpu.HBM)] * 3,
        out_specs=[pl.BlockSpec(memory_space=pltpu.VMEM)] * 2,
        scratch_shapes=[
            pltpu.VMEM((ROUNDS + 2, 2, per, nz, rows[0], channels), BF),
            pltpu.VMEM((ROUNDS + 2, 2, per, nz, rows[1], channels), BF),
            pltpu.VMEM((1, channels), jnp.int32),
            pltpu.VMEM((1, nb), jnp.int32),
            pltpu.VMEM((channels, strain.shape[1]), BF),
            dma((win + 2,)),
            pltpu.VMEM((8 * nb, HOP), BF),
            pltpu.VMEM((channels, channels), BF),
            pltpu.VMEM((win + 3, 2 * nb, channels), F32),
            pltpu.VMEM((channels // 128, nb * rows[0], 128), F32),
            pltpu.VMEM((channels // 128, nb * rows[1], 128), F32),
            pltpu.VMEM((nz, 2, per, rows[0], channels), BF),
            pltpu.VMEM((nz, 2, per, rows[1], channels), BF),
            pltpu.VMEM((2, per, nz, rows[0], channels), BF),
            pltpu.VMEM((2, per, nz, rows[1], channels), BF),
            pltpu.VMEM((3, 2 * nb, channels), BF),
            pltpu.VMEM((3, 2 * nb, channels), BF),
            dma, dma, dma((2,)), dma((nc,)), dma((nc,)), dma((nc, 3)), dma((nc,)), dma((nc, 2)), dma((nc,)), dma((nc, 2)), dma((nc, 2)),
        ],
        compiler_params=pltpu.CompilerParams(
            collective_id=0, has_side_effects=True, vmem_limit_bytes=53_000_000
        ),
        name="exchange",
    )(channel_map, bin_index.reshape(1, nb), strain)

    result = (ROUNDS, per, channels, 2 * channels)
    return pl.pallas_call(
        functools.partial(stacked, 1.0 / math.sqrt(win * nspan)),
        in_specs=[pl.BlockSpec(memory_space=pltpu.VMEM)] * 2,
        out_specs=pl.BlockSpec(memory_space=pl.ANY),
        out_shape=jax.ShapeDtypeStruct(result, BF),
        scratch_shapes=[pltpu.VMEM(result, BF), dma((ROUNDS, per))],
        compiler_params=pltpu.CompilerParams(vmem_limit_bytes=32 * 2**20),
        name="stacked",
    )(left, right)


def solution(mesh):
    return jax.shard_map(
        local,
        mesh=mesh,
        in_specs=(P("grp", "span"), P("grp", None), P()),
        out_specs=P(None, "span", "grp", None),
        check_vma=False,
    )
```

```python
import functools
import math

import jax
import jax.numpy as jnp
from jax import lax
from jax.experimental import pallas as pl
from jax.experimental.pallas import tpu as pltpu
from jax.sharding import PartitionSpec as P

W = 1024
HOP = W // 4
ROUNDS = 3
epsilon = 1e-06
MESH = pl.DeviceIdType.MESH
BF = jnp.bfloat16
F32 = jnp.float32

PART_WINDOWS = (8, 4)
DIRECT = (0,)
CHUNKS = ((0, 0, 1), (0, 1, 1), (1, 0, 2), (0, 2, 1), (1, 2, 2), (0, 3, 1))


def sin_cos(x):
    x2 = x * x
    s = x * (1.0 + x2 * (-1.0 / 6 + x2 * (1.0 / 120 + x2 * (-1.0 / 5040 + x2 * (1.0 / 362880)))))
    c = 1.0 + x2 * (-0.5 + x2 * (1.0 / 24 + x2 * (-1.0 / 720 + x2 * (1.0 / 40320 - x2 * (1.0 / 3628800)))))
    return s, c


def turned(e, s, c):
    odd = (e & 1) == 1
    cos_sign = jnp.where(((e + 1) & 2) == 0, 1.0, -1.0)
    sin_sign = jnp.where((e & 2) == 0, 1.0, -1.0)
    return jnp.where(odd, s, c) * cos_sign, jnp.where(odd, c, s) * sin_sign


def fill_basis(bin_ref, basis):
    nb = bin_ref.shape[1]
    row = lax.broadcasted_iota(jnp.int32, (nb, nb), 0)
    col = lax.broadcasted_iota(jnp.int32, (nb, nb), 1)
    bins = jnp.where(row == col, jnp.broadcast_to(bin_ref[...].astype(F32), (nb, nb)), 0.0)
    bins = jnp.sum(bins, axis=1, keepdims=True).astype(jnp.int32)
    t = lax.broadcasted_iota(jnp.int32, (nb, HOP), 1)
    bins = jnp.broadcast_to(bins, (nb, HOP))

    def parts(m):
        k = (m + 128) >> 8
        s, c = sin_cos((m - (k << 8)).astype(F32) * (2.0 * math.pi / W))
        return k, s, c

    k, s, c = parts((t * bins) & (W - 1))
    tk, ts, tc = parts(lax.broadcasted_iota(jnp.int32, (8, HOP), 1))
    for q in range(4):
        cq, sq = turned((k + q * bins) & 3, s, c)
        tq, _ = turned((tk + q) & 3, ts, tc)
        taper = (0.5 - 0.5 * tq)[:1]
        base = q * 2 * nb
        basis[base : base + nb] = (taper * cq).astype(BF)
        basis[base + nb : base + 2 * nb] = (-taper * sq).astype(BF)


def exchange(
    nz, ngrp, map_hbm, bin_hbm, strain_hbm, left_ref, right_ref,
    slab_a, slab_b, map_ref, bin_ref, strain_ref, load_sem, basis, onehot, wacc, rows_a, rows_b, out_a, out_b, transit_a, transit_b, halo_out, halo_in,
    halo_send, halo_recv, z_send, z_recv, own_sem, x_send, m_recv, x_recv, r_send, l_send, l_recv,
):
    slabs, outs, transits = (slab_a, slab_b), (out_a, out_b), (transit_a, transit_b)
    nspan = 2 * nz
    g, s = lax.axis_index("grp"), lax.axis_index("span")
    z, lo, core = s // 2, s % 2, g % 2
    nb = bin_ref.shape[1]
    channels = strain_ref.shape[0]
    win = strain_ref.shape[1] // HOP

    loads = [
        pltpu.make_async_copy(bin_hbm, bin_ref, load_sem.at[win]),
        pltpu.make_async_copy(map_hbm, map_ref, load_sem.at[win + 1]),
    ]
    for j in range(win):
        hop_samples = (slice(None), slice(j * HOP, (j + 1) * HOP))
        loads.append(pltpu.make_async_copy(strain_hbm.at[hop_samples], strain_ref.at[hop_samples], load_sem.at[j]))
    for load in loads:
        load.start()

    def at(dg, ds):
        return {"grp": lax.rem(g + dg + 2 * ngrp, ngrp), "span": ds}

    behind = lax.rem(s + nspan - 1, nspan)
    ahead = lax.rem(s + 1, nspan)
    other = z * 2 + 1 - lo

    barrier = pltpu.get_barrier_semaphore()

    def hello(device):
        pl.semaphore_signal(barrier, inc=1, device_id=device, device_id_type=MESH)

    hello(at(0, ahead))
    hello(at(0, other))
    quarter = lax.rem(g, 4)
    relayed = jnp.where(quarter == 1, 1, 0)
    relaying = jnp.where(quarter == 3, 1, 0)
    hello(at(2 - 4 * relaying, s))
    hello(at(2 - 4 * relaying, other))

    @pl.when(relaying == 1)
    def _():
        hello(at(4, s))
        hello(at(2, s))
        hello(at(2, other))

    hello(at(1 + 2 * core, s))
    hello(at(1 - 2 * core, s))

    def hello_z(d, _):
        hello(at(0, lax.rem(z + d, nz) * 2 + lo))
        return 0

    lax.fori_loop(1, nz, hello_z, 0)

    loads[0].wait()
    fill_basis(bin_ref, basis)
    loads[1].wait()
    c_in = lax.broadcasted_iota(jnp.int32, (channels, channels), 0)
    onehot[...] = jnp.where(c_in == jnp.broadcast_to(map_ref[...], (channels, channels)), 1.0, 0.0).astype(BF)

    def hop(j):
        loads[2 + j].wait()
        block = strain_ref[:, j * HOP : (j + 1) * HOP]
        part = lax.dot_general(
            basis[...], block, (((1,), (1,)), ((), ())), preferred_element_type=F32
        )
        for q in range(4):
            i = j - q + 3
            piece = part[q * 2 * nb : (q + 1) * 2 * nb]
            if j == 0 or q == 0:
                wacc[i] = piece
            else:
                wacc[i] = wacc[i] + piece

    for j in range(3):
        hop(j)
    halo_out[...] = wacc[0:3].astype(BF)
    pl.semaphore_wait(barrier, nz - 1 + 6 + relaying + 2 * relayed)
    halo = pltpu.make_async_remote_copy(
        src_ref=halo_out, dst_ref=halo_in, send_sem=halo_send, recv_sem=halo_recv,
        device_id=at(0, behind), device_id_type=MESH,
    )
    halo.start()
    for j in range(3, win):
        hop(j)

    def arrange(part, first):
        rows, out = (rows_a, rows_b)[part], outs[part]
        per = 2 * PART_WINDOWS[part]
        for w in range(PART_WINDOWS[part]):
            for p in range(2):
                at_row = (w // 4) * 8 + p * 4 + w % 4
                piece = wacc[3 + first + w, p * nb : (p + 1) * nb, :]
                for h in range(channels // 128):
                    rows[h, pl.ds(at_row, nb, stride=per), :] = piece[:, h * 128 : (h + 1) * 128]
        by_map = jnp.concatenate([rows[h].astype(BF) for h in range(channels // 128)], axis=1)
        ordered = jnp.dot(by_map, onehot[...], preferred_element_type=F32)
        out[...] = ordered.reshape(out.shape).astype(BF)

    def to_slabs(c):
        part, n0, nn = CHUNKS[c]
        out, transit = outs[part], transits[part]
        n = pl.ds(n0, nn)
        pltpu.make_async_copy(out.at[z, :, n], transit.at[:, n, z], z_recv.at[c]).start()

        def step(i, _):
            there = i + jnp.where(i >= z, 1, 0)
            pltpu.make_async_remote_copy(
                src_ref=out.at[there, :, n], dst_ref=transit.at[:, n, z],
                send_sem=z_send.at[part], recv_sem=z_recv.at[c],
                device_id=at(0, there * 2 + lo), device_id_type=MESH,
            ).start()
            return 0

        lax.fori_loop(0, nz - 1, step, 0)

    def arrived(ref, sem):
        pltpu.make_async_copy(ref, ref, sem).wait()

    sent = []

    def send(src, dst, send_sem, recv_sem, device):
        copy = pltpu.make_async_remote_copy(
            src_ref=src, dst_ref=dst, send_sem=send_sem, recv_sem=recv_sem,
            device_id=device, device_id_type=MESH,
        )
        copy.start()
        sent.append(copy)

    def across(c):
        part, n0, nn = CHUNKS[c]
        slab, transit = slabs[part], transits[part]
        n = pl.ds(n0, nn)
        by = 0 if c in DIRECT else relayed
        to, dg, sem = 2 + 2 * by, 4 * by - 2, x_recv.at[c, by]
        arrived(transit.at[:, n], z_recv.at[c])
        send(transit.at[1 - lo, n], slab.at[to, lo, n], x_send.at[c, 1], sem, at(dg, other))
        send(transit.at[1 - lo, n], slab.at[0, lo, n], x_send.at[c, 0], m_recv.at[c], at(0, other))
        send(transit.at[lo, n], slab.at[to, lo, n], x_send.at[c, 2], sem, at(dg, s))
        pltpu.make_async_copy(transit.at[lo, n], slab.at[0, lo, n], own_sem.at[c]).start()

    def relay(c):
        part, n0, nn = CHUNKS[c]
        slab = slabs[part]
        n = pl.ds(n0, nn)

        @pl.when(relaying == 1)
        def _():
            arrived(slab.at[4, :, n], x_recv.at[c, 1])
            pltpu.make_async_remote_copy(
                src_ref=slab.at[4, :, n], dst_ref=slab.at[2, :, n],
                send_sem=r_send.at[c], recv_sem=x_recv.at[c, 0], device_id=at(-4, s), device_id_type=MESH,
            ).start()

    def own_onward(c):
        part, n0, nn = CHUNKS[c]
        slab = slabs[part]
        n = pl.ds(n0, nn)
        arrived(slab.at[0, lo, n], own_sem.at[c])
        arrived(slab.at[0, 1 - lo, n], m_recv.at[c])
        to = 3 - 2 * core
        send(slab.at[0, :, n], slab.at[to, :, n], l_send.at[c, 0], l_recv.at[c, to // 2], at(-to, s))

    def next_onward(c):
        part, n0, nn = CHUNKS[c]
        slab = slabs[part]
        n = pl.ds(n0, nn)
        arrived(slab.at[2, :, n], x_recv.at[c, 0])
        to = 1 + 2 * core
        send(slab.at[2, :, n], slab.at[to, :, n], l_send.at[c, 1], l_recv.at[c, to // 2], at(2 - to, s))

    def last(c):
        part, n0, nn = CHUNKS[c]
        slab = slabs[part]
        n = pl.ds(n0, nn)
        arrived(slab.at[1, :, n], l_recv.at[c, 0])
        arrived(slab.at[3, :, n], l_recv.at[c, 1])

    def whitened(slot, n):
        a = slab_a[slot, :, n].astype(F32)
        b = slab_b[slot, :, n].astype(F32)
        v = jnp.concatenate([a.reshape(-1, channels), b.reshape(-1, channels)], axis=0)
        power = jnp.sum(v * v, axis=0, keepdims=True) * (1.0 / v.shape[0])
        return (v * lax.rsqrt(power + epsilon)).astype(BF)

    def own_bins(*bins):
        for n in bins:
            own = whitened(0, n).astype(F32)
            swapped = pltpu.roll(own.reshape(-1, 8, channels), 4, 1)
            imag_row = lax.broadcasted_iota(jnp.int32, swapped.shape, 1) >= 4
            swapped = jnp.where(imag_row, -swapped, swapped).reshape(own.shape)
            left_ref[n, :channels] = own.T.astype(BF)
            left_ref[n, channels:] = swapped.T.astype(BF)

    def next_bins(slot, *bins):
        for n in bins:
            right_ref[n, slot - 1] = whitened(slot, n)

    arrange(0, 0)
    to_slabs(0)
    to_slabs(1)
    halo.wait()
    keep = jnp.where(s == nspan - 1, 0.0, 1.0)
    for i in range(3):
        wacc[win + i] = wacc[win + i] + halo_in[i].astype(F32) * keep
    arrange(1, PART_WINDOWS[0])
    to_slabs(2)
    to_slabs(3)
    across(0)
    to_slabs(4)
    across(1)
    to_slabs(5)
    own_onward(0)
    across(2)
    relay(1)
    own_onward(1)
    next_onward(0)
    across(3)
    relay(2)
    own_onward(2)
    next_onward(1)
    own_bins(0, 1)
    across(4)
    relay(3)
    own_onward(3)
    next_onward(2)
    across(5)
    relay(4)
    own_onward(4)
    next_onward(3)
    next_bins(2, 0, 1)
    last(0)
    last(1)
    last(2)
    next_bins(1, 0, 1)
    relay(5)
    own_onward(5)
    next_onward(4)
    next_bins(3, 0, 1)
    own_bins(2)
    next_onward(5)
    own_bins(3)
    next_bins(2, 2)
    last(3)
    last(4)
    next_bins(1, 2)
    next_bins(3, 2)
    next_bins(2, 3)
    last(5)
    next_bins(1, 3)
    next_bins(3, 3)
    nc = len(CHUNKS)
    for part in range(2):
        arrived(outs[part].at[pl.ds(0, nz - 1)], z_send.at[part])
    for copy in sent:
        copy.wait_send()

    @pl.when(relaying == 1)
    def _():
        for c in range(nc):
            if c in DIRECT:
                continue
            part, n0, nn = CHUNKS[c]
            ref = slabs[part].at[4, :, pl.ds(n0, nn)]
            arrived(ref, r_send.at[c])


def stacked(scale, left_ref, right_ref, cross_hbm, cross_ref, sem):
    bins, ch = right_ref.shape[0], right_ref.shape[-1]
    copies = []
    for n in range(bins):
        for r in range(ROUNDS):
            both = jnp.dot(left_ref[n], right_ref[n, r], preferred_element_type=F32)
            both = (both * scale).astype(BF)
            cross_ref[r, n, :, :ch] = both[:ch]
            cross_ref[r, n, :, ch:] = both[ch:]
            copy = pltpu.make_async_copy(cross_ref.at[r, n], cross_hbm.at[r, n], sem.at[r, n])
            copy.start()
            copies.append(copy)
    for copy in copies:
        copy.wait()


def local(strain, channel_map, bin_index):
    channels = strain.shape[0]
    nspan, ngrp = lax.axis_size("span"), lax.axis_size("grp")
    nz = nspan // 2
    nb = bin_index.shape[0]
    per = nb // nspan
    rows = [2 * w for w in PART_WINDOWS]
    win = sum(PART_WINDOWS)
    nc = len(CHUNKS)
    dma = pltpu.SemaphoreType.DMA
    depth = nspan * sum(rows)
    left, right = pl.pallas_call(
        functools.partial(exchange, nz, ngrp),
        out_shape=[
            pltpu.VMEM((per, 2 * channels, depth), BF),
            pltpu.VMEM((per, ROUNDS, depth, channels), BF),
        ],
        in_specs=[pl.BlockSpec(memory_space=pltpu.HBM)] * 3,
        out_specs=[pl.BlockSpec(memory_space=pltpu.VMEM)] * 2,
        scratch_shapes=[
            pltpu.VMEM((ROUNDS + 2, 2, per, nz, rows[0], channels), BF),
            pltpu.VMEM((ROUNDS + 2, 2, per, nz, rows[1], channels), BF),
            pltpu.VMEM((1, channels), jnp.int32),
            pltpu.VMEM((1, nb), jnp.int32),
            pltpu.VMEM((channels, strain.shape[1]), BF),
            dma((win + 2,)),
            pltpu.VMEM((8 * nb, HOP), BF),
            pltpu.VMEM((channels, channels), BF),
            pltpu.VMEM((win + 3, 2 * nb, channels), F32),
            pltpu.VMEM((channels // 128, nb * rows[0], 128), F32),
            pltpu.VMEM((channels // 128, nb * rows[1], 128), F32),
            pltpu.VMEM((nz, 2, per, rows[0], channels), BF),
            pltpu.VMEM((nz, 2, per, rows[1], channels), BF),
            pltpu.VMEM((2, per, nz, rows[0], channels), BF),
            pltpu.VMEM((2, per, nz, rows[1], channels), BF),
            pltpu.VMEM((3, 2 * nb, channels), BF),
            pltpu.VMEM((3, 2 * nb, channels), BF),
            dma, dma, dma((2,)), dma((nc,)), dma((nc,)), dma((nc, 3)), dma((nc,)), dma((nc, 2)), dma((nc,)), dma((nc, 2)), dma((nc, 2)),
        ],
        compiler_params=pltpu.CompilerParams(
            collective_id=0, has_side_effects=True, vmem_limit_bytes=53_000_000
        ),
        name="exchange",
    )(channel_map, bin_index.reshape(1, nb), strain)

    result = (ROUNDS, per, channels, 2 * channels)
    return pl.pallas_call(
        functools.partial(stacked, 1.0 / math.sqrt(win * nspan)),
        in_specs=[pl.BlockSpec(memory_space=pltpu.VMEM)] * 2,
        out_specs=pl.BlockSpec(memory_space=pl.ANY),
        out_shape=jax.ShapeDtypeStruct(result, BF),
        scratch_shapes=[pltpu.VMEM(result, BF), dma((ROUNDS, per))],
        compiler_params=pltpu.CompilerParams(vmem_limit_bytes=32 * 2**20),
        name="stacked",
    )(left, right)


def solution(mesh):
    return jax.shard_map(
        local,
        mesh=mesh,
        in_specs=(P("grp", "span"), P("grp", None), P()),
        out_specs=P(None, "span", "grp", None),
        check_vma=False,
    )
```
